256 devices in a mesh: row: 8 (over z_hi, core), col: 32 (over z_lo, x, y).
Axes of the slice: x: 4, y: 4, z: 8 (z_hi: 4, z_lo: 2; z = z_hi * 2 + z_lo), core: 2. Of those that a mesh axis runs over, the one named last changes fastest.
Arguments:
- band_emb: bfloat16 [128, 256], P('row', 'col'), may hold values from -6 to 6
- col_emb: bfloat16 [16384, 256], P('col', 'row'), may hold values from -6 to 6
- w_row: bfloat16 [256, 32], replicated, may hold values from -0.375 to 0.375
- w_col: bfloat16 [256, 32], replicated, may hold values from -0.375 to 0.375
- first_kernel_weight: bfloat16 [32, 32, 3, 3], replicated, may hold values from -0.375 to 0.375
- second_kernel_weight: bfloat16 [32, 32, 3, 3], replicated, may hold values from -0.375 to 0.375
- cotangent: bfloat16 [32, 128, 16384], P(None, 'row', 'col'), may hold values from -6 to 6
- drop_seeds: int32 [8, 32], P('row', 'col'), may hold values from 0 to 16777215
- tile_mask: int32 [8, 32], P('row', 'col'), may hold values from 0 to 1, as said below
- dilations: int32 [2], replicated, may hold values from 1 to 4, as said below
Outputs:
- out_map: bfloat16 [32, 128, 16384], P(None, 'row', 'col')
- grad_band: bfloat16 [128, 256], P('row', 'col')
- grad_cols: bfloat16 [16384, 256], P('col', 'row')
- grad_w_row: float32 [256, 32], replicated
- grad_w_col: float32 [256, 32], replicated
- grad_conv_one: float32 [32, 32, 3, 3], replicated
- grad_conv_two: float32 [32, 32, 3, 3], replicated
The draws below stay inside these ranges and needn't reach their ends.
Inputs may be any that keep to these rules, and one draw needn't show every extreme that they name: `dilations`: one of the two equals 4. For some first bin b0 of the band with b0 >= 512, tile_mask[r, c] is 1 exactly when (c + 1) * 512 > b0 + r * 16.
All inputs are finite; a program needn't handle non-finite values.
Results may differ from the reference program's by a relative error of at most 0.023.
Values may be sent and summed in bfloat16 or wider, within the bound.
No kernel may reach another device: no remote copies, remote signals or barrier semaphores. Data moves between devices by JAX's collectives and lax.ppermute only.
A program may use at most 64 MiB of HBM per device.

```python
import jax
import jax.numpy as jnp
from jax import lax

C = 256
K = 32
LARGEST_SPREAD = 4
TILE_ROW_BINS = 16
COL_DEV = 512
BAND = 128
COLUMN_BINS = 16384


def draw_tile_mask(key, part):
    key = jax.random.fold_in(key, 11)
    start_bin = jax.random.randint(key, (), COL_DEV, COLUMN_BINS - BAND + 1, dtype=jnp.int32)
    block_rows = jnp.arange(BAND // TILE_ROW_BINS, dtype=jnp.int32)[:, None]
    block_cols = jnp.arange(COLUMN_BINS // COL_DEV, dtype=jnp.int32)[None, :]
    return ((block_cols + 1) * COL_DEV > start_bin + block_rows * TILE_ROW_BINS).astype(jnp.int32)


def draw_dilations(key, part):
    key = jax.random.fold_in(key, 12)
    key_value, key_order = jax.random.split(key)
    other_value = jax.random.randint(key_value, (1,), 1, LARGEST_SPREAD + 1, dtype=jnp.int32)
    spacings = jnp.concatenate([jnp.full((1,), LARGEST_SPREAD, jnp.int32), other_value])
    shuffle = jax.random.permutation(key_order, 2)
    return spacings[shuffle]


def place_ends(values, own_key, low, top_value):
    dims = values.shape
    index_at = [jax.random.randint(jax.random.fold_in(own_key, axis), (), 0, dims[axis]) for axis in range(len(dims))]
    values = values.at[tuple(index_at)].set(low)
    longest = dims.index(max(dims))
    index_at[longest] = (index_at[longest] + 1) % dims[longest]
    return values.at[tuple(index_at)].set(top_value)


def levels(own_key, dims, cuts, smallest, high):
    def one(dim, blocks):
        steps = jax.random.uniform(jax.random.fold_in(jax.random.fold_in(own_key, 6), dim), (blocks,), jnp.float32, smallest / len(cuts), high / len(cuts))
        return jnp.repeat(jnp.exp(steps), dims[dim] // blocks).reshape((-1,) + (1,) * (len(dims) - dim - 1))

    level = one(*cuts[0])
    for cut in cuts[1:]:
        level = level * one(*cut)
    return level


def normal_values(key, extent, width, limit, cuts=(), kind=jnp.bfloat16):
    array = jax.random.normal(key, extent, jnp.float32) * width
    if len(cuts) > 0:
        array = levels(key, extent, cuts, -0.22, 0.18) * array
    return jnp.clip(array, min=-limit, max=limit).astype(kind)


def setup_inputs(seed: int = 0) -> dict:
    arg_keys = jax.random.split(jax.random.key(seed), 11)
    band_emb = normal_values(arg_keys[0], (BAND, C), 1.0, 6.0, ((0, 8), (1, 32)))
    col_emb = normal_values(arg_keys[1], (COLUMN_BINS, C), 1.0, 6.0, ((0, 32), (1, 8)))
    w_row = normal_values(arg_keys[2], (C, K), C ** -0.5, 0.375)
    w_col = normal_values(arg_keys[3], (C, K), C ** -0.5, 0.375)
    first_kernel_weight = normal_values(arg_keys[4], (K, K, 3, 3), (9 * K) ** -0.5, 0.375)
    second_kernel_weight = normal_values(arg_keys[5], (K, K, 3, 3), (9 * K) ** -0.5, 0.375)
    cotangent = normal_values(arg_keys[6], (K, BAND, COLUMN_BINS), 1.0, 6.0, ((1, 8), (2, 32)))
    drop_seeds = place_ends(jax.random.randint(arg_keys[7], (BAND // TILE_ROW_BINS, COLUMN_BINS // COL_DEV), 0, 16777216), jax.random.fold_in(arg_keys[7], 1), 0, 16777215).astype(jnp.int32)
    tile_mask = draw_tile_mask(jax.random.fold_in(arg_keys[10], 71), 0)
    dilations = draw_dilations(jax.random.fold_in(arg_keys[10], 71), 0)
    return dict(band_emb=band_emb, col_emb=col_emb, w_row=w_row, w_col=w_col, first_kernel_weight=first_kernel_weight, second_kernel_weight=second_kernel_weight, cotangent=cotangent, drop_seeds=drop_seeds, tile_mask=tile_mask, dilations=dilations)


tanh_scale = 0.7978845608028654
cubic_term = 0.044715
keep_boost = 4.0 / 3.0


def gelu_value(values):
    inner = tanh_scale * (values + cubic_term * values * values * values)
    return 0.5 * values * (1.0 + jnp.tanh(inner))


def gelu_slope(values):
    tangent = jnp.tanh(tanh_scale * (values + cubic_term * values * values * values))
    return 0.5 * (1.0 + tangent) + 0.5 * values * (1.0 - tangent * tangent) * tanh_scale * (1.0 + 3.0 * cubic_term * values * values)


def keep_factor(tile_seed, layer_id, channel, row_ids, col_ids):
    hashed = tile_seed * 1000003 + layer_id * 7919
    hashed = hashed ^ (channel * 73856093)
    hashed = hashed ^ (row_ids * 19349663)
    hashed = hashed ^ (col_ids * 83492791)
    hashed = hashed * 668265261
    hashed = hashed ^ ((hashed >> 15) & 131071)
    hashed = hashed * 374761393
    hashed = hashed ^ ((hashed >> 13) & 524287)
    kept = (hashed & 3) != 0
    return kept.astype(jnp.float32) * keep_boost


def spread_convolution(padded, kernel, spacing, border_rows, out_rows, out_cols):
    def build_branch(spread):
        def convolve(values):
            offset = border_rows - spread
            window = lax.slice(values, (0, offset, offset), (values.shape[0], offset + out_rows + 2 * spread, offset + out_cols + 2 * spread))
            return lax.conv_general_dilated(window[None], kernel, (1, 1), "VALID", rhs_dilation=(spread, spread), dimension_numbers=("NCHW", "OIHW", "NCHW"), preferred_element_type=jnp.float32)[0]
        return convolve
    return lax.switch(spacing - 1, [build_branch(spread) for spread in range(1, border_rows + 1)], padded)


def mirror_kernel(kernel):
    return jnp.transpose(kernel[:, :, ::-1, ::-1], (1, 0, 2, 3))


def kernel_gradient(padded, grads, spacing, border_rows):
    out_rows = grads.shape[1]
    out_cols = grads.shape[2]
    tap_terms = []
    for tap_row in range(3):
        for tap_col in range(3):
            starts = (jnp.zeros((), jnp.int32), (border_rows + (tap_row - 1) * spacing).astype(jnp.int32), (border_rows + (tap_col - 1) * spacing).astype(jnp.int32))
            window = lax.dynamic_slice(padded, starts, (padded.shape[0], out_rows, out_cols))
            tap_terms.append(jnp.einsum("oij,cij->oc", grads, window, preferred_element_type=jnp.float32))
    return jnp.stack(tap_terms, axis=2).reshape(grads.shape[0], padded.shape[0], 3, 3)


def join_blocks(stacked):
    return jnp.moveaxis(stacked, 0, 1).reshape(stacked.shape[1], stacked.shape[0] * stacked.shape[2], stacked.shape[3])


def reference(band_emb, col_emb, w_row, w_col, first_kernel_weight, second_kernel_weight, cotangent, drop_seeds, tile_mask, dilations):
    border_rows = LARGEST_SPREAD
    first_spread = dilations[0]
    second_spread = dilations[1]
    row_proj = jnp.dot(band_emb, w_row, preferred_element_type=jnp.float32)
    col_proj = jnp.dot(col_emb, w_col, preferred_element_type=jnp.float32)
    first_kernel = first_kernel_weight.astype(jnp.float32)
    second_kernel = second_kernel_weight.astype(jnp.float32)
    mirrored_first = mirror_kernel(first_kernel)
    mirrored_second = mirror_kernel(second_kernel)
    channel = jnp.arange(K, dtype=jnp.int32)[:, None, None]
    col_ids = jnp.arange(COLUMN_BINS, dtype=jnp.int32)[None, None, :]
    indices = jnp.arange(BAND // TILE_ROW_BINS, dtype=jnp.int32)

    def keep_mask_for(position_index):
        return jnp.repeat(tile_mask[position_index], COL_DEV).astype(jnp.float32)[None, None, :]

    def factor_of(position_index, layer_id):
        row_ids = (position_index * TILE_ROW_BINS + jnp.arange(TILE_ROW_BINS, dtype=jnp.int32))[None, :, None]
        seed_row = jnp.repeat(drop_seeds[position_index], COL_DEV)[None, None, :]
        return keep_mask_for(position_index) * keep_factor(seed_row, layer_id, channel, row_ids, col_ids)

    def rows_for_device(padded, position_index):
        return lax.dynamic_slice_in_dim(padded, position_index * TILE_ROW_BINS, TILE_ROW_BINS + 2 * border_rows, 1).astype(jnp.float32)

    def unpadded_rows(values, position_index):
        return lax.dynamic_slice_in_dim(values, position_index * TILE_ROW_BINS, TILE_ROW_BINS, 1).astype(jnp.float32)

    def pad_map(values):
        return jnp.pad(values, ((0, 0), (border_rows, border_rows), (border_rows, border_rows)))

    def pair_block(position_index):
        row_part = lax.dynamic_slice_in_dim(row_proj, position_index * TILE_ROW_BINS, TILE_ROW_BINS, 0)
        summed = row_part.T[:, :, None] + col_proj.T[:, None, :]
        return (keep_mask_for(position_index) * summed).astype(jnp.bfloat16)

    pair_map = join_blocks(lax.map(pair_block, indices))
    pair_padded = pad_map(pair_map)

    def first_block(position_index):
        first_preactivation = spread_convolution(rows_for_device(pair_padded, position_index), first_kernel, first_spread, border_rows, TILE_ROW_BINS, COLUMN_BINS)
        return (factor_of(position_index, 1) * gelu_value(first_preactivation)).astype(jnp.bfloat16)

    hidden = join_blocks(lax.map(first_block, indices))
    hidden_padded = pad_map(hidden)

    def second_block(position_index):
        second_preactivation = spread_convolution(rows_for_device(hidden_padded, position_index), second_kernel, second_spread, border_rows, TILE_ROW_BINS, COLUMN_BINS)
        factor_two = factor_of(position_index, 2)
        result = (factor_two * gelu_value(second_preactivation)).astype(jnp.bfloat16)
        second_gradient = (unpadded_rows(cotangent, position_index) * factor_two * gelu_slope(second_preactivation)).astype(jnp.bfloat16)
        return result, second_gradient

    out_stack, grad_two_stack = lax.map(second_block, indices)
    out_map = join_blocks(out_stack)
    second_gradient = join_blocks(grad_two_stack)
    second_gradient_padded = pad_map(second_gradient)

    def third_block(position_index):
        first_preactivation = spread_convolution(rows_for_device(pair_padded, position_index), first_kernel, first_spread, border_rows, TILE_ROW_BINS, COLUMN_BINS)
        hidden_gradient = spread_convolution(rows_for_device(second_gradient_padded, position_index), mirrored_second, second_spread, border_rows, TILE_ROW_BINS, COLUMN_BINS)
        first_gradient = (hidden_gradient * factor_of(position_index, 1) * gelu_slope(first_preactivation)).astype(jnp.bfloat16)
        kernel_share = kernel_gradient(rows_for_device(hidden_padded, position_index), unpadded_rows(second_gradient, position_index), second_spread, border_rows)
        return first_gradient, kernel_share

    grad_one_stack, kernel_two_parts = lax.map(third_block, indices)
    first_gradient = join_blocks(grad_one_stack)
    first_gradient_padded = pad_map(first_gradient)

    def fourth_block(position_index):
        pair_gradient = keep_mask_for(position_index) * spread_convolution(rows_for_device(first_gradient_padded, position_index), mirrored_first, first_spread, border_rows, TILE_ROW_BINS, COLUMN_BINS)
        kernel_share = kernel_gradient(rows_for_device(pair_padded, position_index), unpadded_rows(first_gradient, position_index), first_spread, border_rows)
        return jnp.sum(pair_gradient, axis=2).T, jnp.sum(pair_gradient, axis=1).T, kernel_share

    row_stack, col_stack, kernel_one_parts = lax.map(fourth_block, indices)
    row_sum = row_stack.reshape(BAND, K)
    col_sum = jnp.sum(col_stack, axis=0)
    grad_conv_one = jnp.sum(kernel_one_parts, axis=0)
    grad_conv_two = jnp.sum(kernel_two_parts, axis=0)
    highest = lax.Precision.HIGHEST
    grad_w_row = jnp.dot(band_emb.astype(jnp.float32).T, row_sum, precision=highest)
    grad_w_col = jnp.dot(col_emb.astype(jnp.float32).T, col_sum, precision=highest)
    grad_band = jnp.dot(row_sum, w_row.astype(jnp.float32).T, precision=highest).astype(jnp.bfloat16)
    grad_cols = jnp.dot(col_sum, w_col.astype(jnp.float32).T, precision=highest).astype(jnp.bfloat16)
    return (out_map, grad_band, grad_cols, grad_w_row, grad_w_col, grad_conv_one, grad_conv_two)
```

```python
import functools

import jax
import jax.numpy as jnp
from jax import lax
from jax.experimental import pallas as pl
from jax.experimental.pallas import tpu as pltpu
from jax.sharding import PartitionSpec as P

tanh_scale = 0.7978845608028654
cubic_term = 0.044715
keep_boost = 4.0 / 3.0
slope_cubic = 3.0 * tanh_scale * cubic_term

K = 32
ROWS = 16
COLS = 512
WIDE = 640
TAPS = 9
BLK = 8 * K
HIGH = lax.Precision.HIGHEST
f32 = jnp.float32
bf16 = jnp.bfloat16
VMEM_LIMIT = 56 * 1024 * 1024


def dot(a, b, precision=None):
    return lax.dot_general(
        a, b, (((1,), (0,)), ((), ())), precision=precision, preferred_element_type=f32
    )


def dot_nt(a, b, precision=None):
    return lax.dot_general(
        a, b, (((1,), (1,)), ((), ())), precision=precision, preferred_element_type=f32
    )


def dot_tn(a, b, precision=None):
    return lax.dot_general(
        a, b, (((0,), (0,)), ((), ())), precision=precision, preferred_element_type=f32
    )


def iota(shape, dim):
    return lax.broadcasted_iota(jnp.int32, shape, dim)


def ahead(x, s):
    lane = iota((x.shape[0], 128), 1)
    turned = [pltpu.roll(x[:, i : i + 128], 128 - s, 1) for i in range(0, x.shape[1], 128)]
    nxt = turned[1:] + turned[:1]
    return jnp.concatenate(
        [jnp.where(lane >= 128 - s, n, t) for t, n in zip(turned, nxt)], axis=1
    )


def behind(x, s):
    lane = iota((x.shape[0], 128), 1)
    turned = [pltpu.roll(x[:, i : i + 128], s, 1) for i in range(0, x.shape[1], 128)]
    prv = turned[-1:] + turned[:-1]
    return jnp.concatenate([jnp.where(lane < s, p, t) for t, p in zip(turned, prv)], axis=1)


def mixed(base, factor):
    h = base * 668265261
    h = h ^ lax.shift_right_logical(h, 15)
    h = h * 374761393
    h = h ^ lax.shift_right_logical(h, 13)
    return jnp.where((h & 3) != 0, factor, 0.0)


def gelu_parts(v):
    v2 = v * v
    t = jnp.tanh(v * (tanh_scale + (tanh_scale * cubic_term) * v2))
    p = 0.5 + 0.5 * t
    value = v * p
    slope = p + value * (1.0 - t) * (tanh_scale + slope_cubic * v2)
    return value, slope


def pack_kernel(place, got_ref, cols_ref, out_ref):
    c = place[3]
    left = got_ref[lax.rem(c + 31, 32)].astype(f32)
    right = got_ref[lax.rem(c + 1, 32)].astype(f32)
    own = got_ref[c].astype(f32)
    lane = iota((16, 128), 1)
    low = jnp.where(lane < 64, right, left)
    high = jnp.where(
        lane < 16,
        pltpu.roll(right, 128 - 16, 1),
        jnp.where(lane < 112, own, pltpu.roll(left, 16, 1)),
    )
    out_ref[:, :COLS] = cols_ref[...]
    out_ref[:, COLS:WIDE] = jnp.concatenate([low, high], axis=0).astype(bf16)
    features = got_ref[...].astype(f32)[:, 0:8, :].reshape(256, 128).astype(bf16)
    pick = (iota((16, 128), 1) == iota((16, 128), 0) + 64).astype(f32).astype(bf16)
    band = dot_nt(pick, features)
    out_ref[:, WIDE:] = jnp.concatenate([band[:, :128], band[:, 128:]], axis=0).astype(bf16)


def main_kernel(
    place,
    got_ref,
    wr_ref,
    wc_ref,
    w1_ref,
    w2_ref,
    cot_ref,
    cot_up_ref,
    cot_down_ref,
    out_ref,
    send_ref,
    rowsum_ref,
    t1,
    t2,
    t2m,
    pv,
    hv,
    gv,
    g1,
    d1,
    acc,
    first_out,
    row3,
    qv,
    keep_rows,
    seed_rows,
    base_ref,
    keep_ref,
):
    s1 = place[0]
    s2 = place[1]
    r = place[2]
    c = place[3]

    spread = (iota((K, BLK), 1) // 8 == iota((K, BLK), 0)).astype(f32).astype(bf16)
    sub = iota((8, BLK), 0)
    far = iota((8, BLK), 1) % 8 - sub

    def hits(s, half):
        return [far + 8 * half == 4 + (a - 1) * s for a in range(3)]

    def build(target, weight, s, mirrored):
        masks = [hits(s, half) for half in range(2)]
        for b in range(3):
            grown = []
            for a in range(3):
                if mirrored:
                    grown.append(dot_tn(weight[(2 - a) * 3 + (2 - b)], spread))
                else:
                    grown.append(dot(weight[a * 3 + b], spread))
            for half in range(2):
                m = masks[half]
                whole = jnp.zeros((K, 8, BLK), f32)
                for a in range(3):
                    whole = jnp.where(
                        jnp.broadcast_to(m[a][None], (K, 8, BLK)),
                        jnp.broadcast_to(grown[a][:, None, :], (K, 8, BLK)),
                        whole,
                    )
                at = (half * 3 + b) * BLK
                target[:, at : at + BLK] = whole.reshape(BLK, BLK).astype(bf16)

    build(t1, w1_ref, s1, False)
    build(t2, w2_ref, s2, False)
    build(t2m, w2_ref, s2, True)

    q = jnp.zeros((K, WIDE), f32)
    for slot in range(8):
        at = place[4 + slot]
        weight = wc_ref[pl.ds(pl.multiple_of(at * K, K), K), :]
        q = q + dot_tn(weight, got_ref[slot, :, 0:WIDE])
    qv[0] = behind(q, s1)
    qv[1] = q
    qv[2] = ahead(q, s1)

    lane = iota((1, WIDE), 1)
    for step in range(3):
        slot = place[12 + step]
        low = wr_ref[0:128, :]
        high = wr_ref[128:256, :]
        row3[16 * step : 16 * step + 16, :] = dot(
            got_ref[slot, 0:16, WIDE:], low
        ) + dot(got_ref[slot, 16:32, WIDE:], high)
        seen = got_ref[slot, :, COLS:WIDE].astype(f32)
        sides = []
        for row, first in ((24, 32), (8, 32), (8, 64)):
            piece = seen[row : row + 1, first : first + 4]
            number = piece[:, 0:1] * 65536.0 + piece[:, 1:2] * 256.0 + piece[:, 2:3]
            sides.append((number, piece[:, 3:4]))
        row_ok = jnp.logical_and(r + step >= 1, r + step <= 8).astype(f32)
        right_ok = row_ok * (c < 31).astype(f32)
        left_ok = row_ok * (c > 0).astype(f32)
        keep = jnp.where(
            lane < COLS,
            sides[0][1] * row_ok,
            jnp.where(lane < 576, sides[1][1] * right_ok, sides[2][1] * left_ok),
        )
        seed = jnp.where(
            lane < COLS, sides[0][0], jnp.where(lane < 576, sides[1][0], sides[2][0])
        )
        seed_rows[step] = seed.astype(jnp.int32)
        keep_rows[step * 3 + 0] = behind(keep, s1)
        keep_rows[step * 3 + 1] = keep
        keep_rows[step * 3 + 2] = ahead(keep, s1)

    def pair_block(k, carry):
        rows = row3[pl.ds(pl.multiple_of(8 * k, 8), 8), :]
        step = k // 2
        for b in range(3):
            keep = keep_rows[step * 3 + b]
            for p in range(K // 2):
                parts = []
                for ch in (2 * p, 2 * p + 1):
                    parts.append(keep * (rows[:, ch : ch + 1] + qv[b, ch : ch + 1, :]))
                at = pl.multiple_of(k * 3 * BLK + b * BLK + 16 * p, 16)
                pv[pl.ds(at, 16), :] = jnp.concatenate(parts, axis=0).astype(bf16)
        return carry

    lax.fori_loop(0, 6, pair_block, 0)

    column = iota((8, WIDE), 1)
    column = c * COLS + jnp.where(column < 576, column, column - WIDE)

    def prepare(first_row, layer):
        local = first_row + iota((8, WIDE), 0)
        seed = jnp.where(
            local < 0, seed_rows[0], jnp.where(local < ROWS, seed_rows[1], seed_rows[2])
        )
        keep = jnp.where(
            local < 0, keep_rows[1], jnp.where(local < ROWS, keep_rows[4], keep_rows[7])
        )
        base = seed * 1000003 + layer * 7919
        base = base ^ ((r * ROWS + local) * 19349663)
        base_ref[...] = base ^ (column * 83492791)
        keep_ref[...] = keep * keep_boost

    def factor_of(p):
        keep = keep_ref[...]
        base = base_ref[...]
        parts = [mixed(base ^ (ch * 73856093), keep) for ch in (2 * p, 2 * p + 1)]
        return jnp.concatenate(parts, axis=0)

    def store_shifted(target, block, p, values, s):
        for b, moved in enumerate((behind(values, s), values, ahead(values, s))):
            at = pl.multiple_of(block * 3 * BLK + b * BLK + 16 * p, 16)
            target[pl.ds(at, 16), :] = moved.astype(bf16)

    for k in range(5):
        acc[...] = dot(t1[...], pv[k * 3 * BLK : (k + 2) * 3 * BLK, :])
        prepare(8 * k - 12, 1)

        def hidden_pair(p, carry, k=k):
            at = pl.multiple_of(16 * p, 16)
            value, slope = gelu_parts(acc[pl.ds(at, 16), :])
            factor = factor_of(p)
            store_shifted(hv, k, p, factor * value, s2)
            if 1 <= k <= 3:
                d1[pl.ds(pl.multiple_of((k - 1) * BLK + 16 * p, 16), 16), :] = factor * slope
            return carry

        lax.fori_loop(0, K // 2, hidden_pair, 0, unroll=4)

    for k in range(4):
        acc[...] = dot(t2[...], hv[k * 3 * BLK : (k + 2) * 3 * BLK, :])
        prepare(8 * k - 8, 2)

        def grad_pair_of(p, carry, k=k):
            at = pl.multiple_of(16 * p, 16)
            value, slope = gelu_parts(acc[pl.ds(at, 16), :])
            factor = factor_of(p)
            if k == 0:
                cot = cot_up_ref[pl.ds(at, 16), :].astype(f32)
            elif k == 3:
                cot = cot_down_ref[pl.ds(at, 16), :].astype(f32)
            else:
                parts = []
                for ch in (2 * p, 2 * p + 1):
                    parts.append(cot_ref[ch].astype(f32)[8 * (k - 1) : 8 * k])
                cot = jnp.concatenate(parts, axis=0)
            store_shifted(gv, k, p, cot * factor * slope, s2)
            if k == 1:
                first_out[pl.ds(at, 16), :] = (factor * value)[:, :COLS]
            if k == 2:
                upper = first_out[pl.ds(at, 16), :]
                lower = (factor * value)[:, :COLS]
                for i in range(2):
                    both = jnp.concatenate(
                        [upper[8 * i : 8 * i + 8], lower[8 * i : 8 * i + 8]], axis=0
                    )
                    out_ref[2 * p + i] = both.astype(bf16)
            return carry

        lax.fori_loop(0, K // 2, grad_pair_of, 0, unroll=4)

    for k in range(3):
        hidden_grad = dot(t2m[...], gv[k * 3 * BLK : (k + 2) * 3 * BLK, :])
        g1[k * BLK : (k + 1) * BLK, :] = (hidden_grad * d1[k * BLK : (k + 1) * BLK, :]).astype(
            bf16
        )

    crossed = []
    for half in range(2):
        total = jnp.zeros((BLK, 3 * BLK), f32)
        for k in (1, 2):
            start = k * 3 * BLK + BLK
            grads = gv[start : start + BLK, 0:COLS]
            start = (k + half) * 3 * BLK
            total = total + dot_nt(grads, hv[start : start + 3 * BLK, 0:COLS])
        crossed.append(total)
    gather8 = (iota((3 * BLK, 96), 0) // 8 == iota((3 * BLK, 96), 1)).astype(f32)
    masks = [hits(s2, half) for half in range(2)]
    second_rows = []
    for a in range(3):
        found = jnp.zeros((K, 8, 3 * BLK), f32)
        for half in range(2):
            m = jnp.concatenate([masks[half][a].astype(f32)] * 3, axis=1)
            found = found + crossed[half].reshape(K, 8, 3 * BLK) * m[None]
        second_rows.append(dot(jnp.sum(found, axis=1), gather8, HIGH))
    second_total = jnp.concatenate(second_rows, axis=0)

    place_j = iota((WIDE, 384), 0)
    place_j = jnp.where(place_j < 576, place_j, place_j - WIDE)
    moved_j = place_j + (iota((WIDE, 384), 1) // 128 - 1) * s1
    window = jnp.logical_and(moved_j >= 0, moved_j < COLS).astype(f32).astype(bf16)
    by_row = dot(g1[...], window)
    which = iota((3 * BLK, 384), 0)
    which = which // BLK * 8 + which % 8
    by_row = jnp.where(iota((3 * BLK, 384), 1) % 128 == which, by_row, 0.0)
    same = (iota((K, 3 * BLK), 1) % BLK // 8 == iota((K, 3 * BLK), 0)).astype(f32)
    by_row = dot(same, by_row, HIGH)
    across = iota((96, 3 * BLK), 1)
    down = iota((96, 3 * BLK), 0)
    moved_i = across // BLK * 8 + across % 8 - 4 + (down // K - 1) * s1
    inside = jnp.logical_and(moved_i >= 0, moved_i < ROWS)
    inside = jnp.logical_and(inside, across % BLK // 8 == down % K)
    by_col = dot(inside.astype(f32).astype(bf16), g1[...])
    by_col = [ahead(by_col, s1), by_col, behind(by_col, s1)]

    keep_own = keep_rows[4][:, 0:1]
    slot = place[13]
    band = jnp.concatenate([got_ref[slot, 0:16, WIDE:], got_ref[slot, 16:32, WIDE:]], axis=1)
    row_t = dot_tn(wr_ref[...], jnp.concatenate([band.T, jnp.zeros((256, 112), bf16)], axis=1))

    col_sum = jnp.zeros((K, WIDE), f32)
    row_sum = jnp.zeros((K, 128), f32)
    first_cols = []
    row_taps = []
    for a in range(3):
        seen = jnp.zeros((K, 128), f32)
        for b in range(3):
            seen = seen + dot_tn(
                w1_ref[a * 3 + b].astype(f32), by_row[:, 128 * b : 128 * b + 128], HIGH
            )
        row_sum = row_sum + pltpu.roll(seen, 128 - (4 - (a - 1) * s1), 1)
    for b in range(3):
        flat = jnp.concatenate([w1_ref[a * 3 + b] for a in range(3)], axis=0).astype(f32)
        col_sum = col_sum + dot_tn(flat, by_col[b], HIGH)
        from_cols = dot_nt(by_col[b][:, :COLS], q[:, :COLS], HIGH)
        from_rows = []
        for a in range(3):
            moved = pltpu.roll(by_row[:, 128 * b : 128 * b + 128], 128 - (4 - (a - 1) * s1), 1)
            from_rows.append(dot_nt(moved, row_t, HIGH))
        first_cols.append(from_cols + jnp.concatenate(from_rows, axis=0))
    first_total = jnp.concatenate(first_cols, axis=1) * keep_own
    rowsum_ref[...] = row_sum * keep_own

    col_sum = (col_sum * keep_own).astype(bf16)
    blank = jnp.zeros((96, 32), f32)
    both = jnp.concatenate(
        [
            jnp.concatenate([first_total, blank], axis=1),
            jnp.concatenate([second_total, blank], axis=1),
        ],
        axis=0,
    )
    for to in range(8):
        for g in range(4):
            send_ref[to, 32 * g : 32 * g + 32, :] = col_sum[:, 128 * g : 128 * g + 128]
        piece = jnp.concatenate([both[24 * to : 24 * to + 24], jnp.zeros((8, 128), f32)], axis=0)
        send_ref[to, 128:160, :] = piece.astype(bf16)


def middle_kernel(place, got_ref, cols_ref, wc_ref, rowsum_ref, gcols_ref, send_ref):
    r = place[2]
    total = got_ref[0].astype(f32)
    for i in range(1, 8):
        total = total + got_ref[i].astype(f32)
    weight = wc_ref[pl.ds(pl.multiple_of(r * K, K), K), :].astype(f32)
    grad_w = jnp.zeros((K, K), f32)
    for g in range(4):
        part = total[32 * g : 32 * g + 32, :]
        gcols_ref[:, 128 * g : 128 * g + 128] = dot(weight, part, HIGH).astype(bf16)
        grad_w = grad_w + dot_nt(cols_ref[:, 128 * g : 128 * g + 128].astype(f32), part, HIGH)
    packed = jnp.concatenate([grad_w[8 * g : 8 * g + 8] for g in range(4)], axis=1)
    send_ref[:, 0:128] = jnp.concatenate([total[128:152], packed], axis=0)
    send_ref[:, 128:256] = rowsum_ref[...]


def sum_kernel(got_ref, send_ref):
    line = jnp.sum(got_ref[...], axis=0, keepdims=True)
    send_ref[...] = jnp.broadcast_to(line[None], send_ref.shape)


def last_kernel(place, got_ref, all_ref, wr_ref, gband_ref, gwr_ref, gwc_ref, g1_ref, g2_ref):
    r = place[2]
    c = place[3]
    pieces = [got_ref[i] for i in range(8)]
    whole = jnp.concatenate([piece[0:24, 0:128] for piece in pieces], axis=0)
    for a in range(3):
        for b in range(3):
            g1_ref[a * 3 + b] = whole[32 * a : 32 * a + 32, 32 * b : 32 * b + 32]
            g2_ref[a * 3 + b] = whole[96 + 32 * a : 128 + 32 * a, 32 * b : 32 * b + 32]
    gwr = jnp.zeros((K, 256), f32)
    gwc = []
    for i in range(8):
        for g in range(4):
            gwc.append(pieces[i][24:32, 32 * g : 32 * g + 32])
    gwc_ref[...] = jnp.concatenate(gwc, axis=0)
    for slot in range(8):
        at = place[4 + slot]
        rows = got_ref[at, :, 128:144]
        low = dot(rows, all_ref[slot, 0:16, WIDE:].astype(f32), HIGH)
        high = dot(rows, all_ref[slot, 16:32, WIDE:].astype(f32), HIGH)
        gwr = gwr + jnp.concatenate([low, high], axis=1)
    gwr_ref[...] = gwr
    mine = wr_ref[pl.ds(pl.multiple_of(c * 8, 8), 8), :]
    gband_ref[...] = dot(mine, got_ref[r, :, 128:144], HIGH).astype(bf16)


def spaces(count, with_place=True):
    whole = [pl.BlockSpec(memory_space=pltpu.VMEM)] * count
    if with_place:
        return [pl.BlockSpec(memory_space=pltpu.SMEM)] + whole
    return whole


def call(kernel, shapes, args, scratch=(), with_place=True):
    return pl.pallas_call(
        kernel,
        out_shape=shapes,
        in_specs=spaces(len(args) - int(with_place), with_place),
        out_specs=jax.tree.map(lambda _: pl.BlockSpec(memory_space=pltpu.VMEM), shapes),
        scratch_shapes=list(scratch),
        compiler_params=pltpu.CompilerParams(vmem_limit_bytes=VMEM_LIMIT),
    )(*args)


def shape(dims, kind):
    return jax.ShapeDtypeStruct(dims, kind)


def per_device(
    band_emb,
    col_emb,
    w_row,
    w_col,
    first_kernel_weight,
    second_kernel_weight,
    cotangent,
    drop_seeds,
    tile_mask,
    dilations,
):
    r = lax.axis_index("row")
    c = lax.axis_index("col")
    rows = lax.axis_size("row")
    cols = lax.axis_size("col")
    order = jnp.arange(8, dtype=jnp.int32)
    around = jnp.stack([(r + 7) % 8, r, (r + 1) % 8]).astype(jnp.int32)
    place = jnp.concatenate(
        [dilations, jnp.stack([r, c]).astype(jnp.int32), order, around, jnp.zeros((1,), jnp.int32)]
    )

    east = [(i, (i + 1) % cols) for i in range(cols - 1)]
    west = [(j, i) for i, j in east]
    south = [(i, (i + 1) % rows) for i in range(rows - 1)]
    north = [(j, i) for i, j in south]
    right = lax.ppermute(cotangent[:, :, :8], "col", west)
    left = lax.ppermute(cotangent[:, :, COLS - 8 :], "col", east)

    cols_t = col_emb.T
    seed = drop_seeds.reshape(1, 1)
    numbers = jnp.concatenate(
        [seed >> 16 & 255, seed >> 8 & 255, seed & 255, tile_mask.reshape(1, 1)], axis=1
    ).astype(bf16)
    edge = jnp.zeros((16, 128), bf16)
    edge = edge.at[:, 0:16].set(cols_t[0:16, 0:16])
    edge = edge.at[:, 16:32].set(cols_t[16:32, 0:16])
    edge = edge.at[8:9, 32:36].set(numbers)
    edge = edge.at[8:9, 64:68].set(numbers)
    edge = edge.at[0:8, 64:80].set(band_emb.T)
    edge = edge.at[:, 96:112].set(cols_t[16:32, COLS - 16 :])
    edge = edge.at[:, 112:128].set(cols_t[0:16, COLS - 16 :])
    got = lax.all_to_all(jnp.broadcast_to(edge[None], (32, 16, 128)), "col", 0, 0)
    packed = call(pack_kernel, shape((32, 768), bf16), (place, got, cols_t))

    gap = jnp.zeros((K, ROWS, 112), bf16)
    cot_ext = jnp.concatenate([cotangent, right, gap, left], axis=2)
    cot_up = lax.ppermute(cot_ext[:, 8:, :].reshape(BLK, WIDE), "row", south)
    cot_down = lax.ppermute(cot_ext[:, :8, :].reshape(BLK, WIDE), "row", north)

    features = lax.all_to_all(jnp.broadcast_to(packed[None], (8, 32, 768)), "row", 0, 0)

    w1 = jnp.transpose(first_kernel_weight, (2, 3, 0, 1)).reshape(TAPS, K, K)
    w2 = jnp.transpose(second_kernel_weight, (2, 3, 0, 1)).reshape(TAPS, K, K)
    out_map, sums, row_sum = call(
        main_kernel,
        (
            shape((K, ROWS, COLS), bf16),
            shape((8, 160, 128), bf16),
            shape((K, 128), f32),
        ),
        (place, features, w_row, w_col, w1, w2, cot_ext, cot_up, cot_down),
        scratch=(
            pltpu.VMEM((BLK, 6 * BLK), bf16),
            pltpu.VMEM((BLK, 6 * BLK), bf16),
            pltpu.VMEM((BLK, 6 * BLK), bf16),
            pltpu.VMEM((18 * BLK, WIDE), bf16),
            pltpu.VMEM((15 * BLK, WIDE), bf16),
            pltpu.VMEM((12 * BLK, WIDE), bf16),
            pltpu.VMEM((3 * BLK, WIDE), bf16),
            pltpu.VMEM((3 * BLK, WIDE), f32),
            pltpu.VMEM((BLK, WIDE), f32),
            pltpu.VMEM((BLK, COLS), f32),
            pltpu.VMEM((48, K), f32),
            pltpu.VMEM((3, K, WIDE), f32),
            pltpu.VMEM((9, 1, WIDE), f32),
            pltpu.VMEM((3, 1, WIDE), jnp.int32),
            pltpu.VMEM((8, WIDE), jnp.int32),
            pltpu.VMEM((8, WIDE), f32),
        ),
    )

    got = lax.all_to_all(sums, "row", 0, 0)
    grad_cols, terms = call(
        middle_kernel,
        (shape((K, COLS), bf16), shape((32, 256), f32)),
        (place, got, cols_t, w_col, row_sum),
    )
    got = lax.all_to_all(terms, "col", 0, 0, tiled=True)
    line = call(sum_kernel, shape((256, 1, 256), f32), (got,), with_place=False)
    got = lax.all_to_all(line, ("row", "col"), 0, 0, tiled=True).reshape(8, 32, 256)
    grad_band, grad_w_row, grad_w_col, grad_one, grad_two = call(
        last_kernel,
        (
            shape((8, ROWS), bf16),
            shape((K, 256), f32),
            shape((256, K), f32),
            shape((TAPS, K, K), f32),
            shape((TAPS, K, K), f32),
        ),
        (place, got, features, w_row.astype(f32)),
    )
    unfold = lambda x: jnp.transpose(x.reshape(3, 3, K, K), (2, 3, 0, 1))
    return (
        out_map,
        grad_band.T,
        grad_cols.T,
        grad_w_row.T,
        grad_w_col,
        unfold(grad_one),
        unfold(grad_two),
    )


def solution(mesh):
    placed = (
        P("row", "col"),
        P("col", "row"),
        P(),
        P(),
        P(),
        P(),
        P(None, "row", "col"),
        P("row", "col"),
        P("row", "col"),
        P(),
    )
    return jax.shard_map(
        per_device,
        mesh=mesh,
        in_specs=placed,
        out_specs=(P(None, "row", "col"), P("row", "col"), P("col", "row"), P(), P(), P(), P()),
        check_vma=False,
    )
```

```python
import functools

import jax
import jax.numpy as jnp
from jax import lax
from jax.experimental import pallas as pl
from jax.experimental.pallas import tpu as pltpu
from jax.sharding import PartitionSpec as P

tanh_scale = 0.7978845608028654
cubic_term = 0.044715
keep_boost = 4.0 / 3.0
slope_cubic = 3.0 * tanh_scale * cubic_term

K = 32
ROWS = 16
COLS = 512
WIDE = 640
TAPS = 9
BLK = 8 * K
HIGH = lax.Precision.HIGHEST
f32 = jnp.float32
bf16 = jnp.bfloat16
VMEM_LIMIT = 56 * 1024 * 1024


def dot(a, b, precision=None):
    return lax.dot_general(
        a, b, (((1,), (0,)), ((), ())), precision=precision, preferred_element_type=f32
    )


def dot_nt(a, b, precision=None):
    return lax.dot_general(
        a, b, (((1,), (1,)), ((), ())), precision=precision, preferred_element_type=f32
    )


def dot_tn(a, b, precision=None):
    return lax.dot_general(
        a, b, (((0,), (0,)), ((), ())), precision=precision, preferred_element_type=f32
    )


def iota(shape, dim):
    return lax.broadcasted_iota(jnp.int32, shape, dim)


def ahead(x, s):
    lane = iota((x.shape[0], 128), 1)
    turned = [pltpu.roll(x[:, i : i + 128], 128 - s, 1) for i in range(0, x.shape[1], 128)]
    nxt = turned[1:] + turned[:1]
    return jnp.concatenate(
        [jnp.where(lane >= 128 - s, n, t) for t, n in zip(turned, nxt)], axis=1
    )


def behind(x, s):
    lane = iota((x.shape[0], 128), 1)
    turned = [pltpu.roll(x[:, i : i + 128], s, 1) for i in range(0, x.shape[1], 128)]
    prv = turned[-1:] + turned[:-1]
    return jnp.concatenate([jnp.where(lane < s, p, t) for t, p in zip(turned, prv)], axis=1)


def mixed(base, factor):
    h = base * 668265261
    h = h ^ lax.shift_right_logical(h, 15)
    h = h * 374761393
    h = h ^ lax.shift_right_logical(h, 13)
    return jnp.where((h & 3) != 0, factor, 0.0)


def wrapped(number):
    return (number + 2**31) % 2**32 - 2**31


def gelu_parts(v):
    v2 = v * v
    t = jnp.tanh(v * (tanh_scale + (tanh_scale * cubic_term) * v2))
    p = 0.5 + 0.5 * t
    value = v * p
    slope = p + value * (1.0 - t) * (tanh_scale + slope_cubic * v2)
    return value, slope


def first_kernel(seed_ref, mask_ref, cols_ref, band_ref, out_ref):
    out_ref[0:32, :] = cols_ref[...]
    lane = iota((8, 128), 1)
    seed = seed_ref[0, 0]
    bytes_of = [seed >> 16 & 255, seed >> 8 & 255, seed & 255, mask_ref[0, 0]]
    numbers = jnp.zeros((8, 128), jnp.int32)
    for i, value in enumerate(bytes_of):
        numbers = jnp.where(lane == i, value, numbers)
    band = jnp.concatenate([band_ref[...].astype(f32), jnp.zeros((8, 112), f32)], axis=1)
    out_ref[32:48, 0:128] = jnp.concatenate([band, numbers.astype(f32)], axis=0).astype(bf16)
    out_ref[32:48, 128:] = jnp.zeros((16, COLS - 128), bf16)


def pack_kernel(
    own_ref, one_ref, two_ref, three_ref, other_ref, cot_ref, up_ref, down_ref,
    feats_ref, west_ref, east_ref, bands_ref,
):
    even = lax.rem(lax.axis_index("row"), 2) == 0
    lane = iota((32, 128), 1)
    mine = [own_ref, one_ref, two_ref, three_ref]
    west = jnp.zeros((32, 128), f32)
    east = jnp.zeros((32, 128), f32)
    bands = jnp.zeros((8, 128), f32)
    seeds = jnp.zeros((8, 128), f32)
    for t in range(8):
        a = mine[t // 2]
        b = other_ref.at[t // 2]
        if t % 2 == 0:
            pick = lambda rows, cols: jnp.where(even, a[rows, cols], b[rows, cols])
        else:
            pick = lambda rows, cols: jnp.where(even, b[rows, cols], a[rows, cols])
        feats_ref[t] = pick(slice(0, 32), slice(0, COLS))
        here = jnp.logical_and(lane >= 16 * t, lane < 16 * t + 16)
        first = pick(slice(0, 32), slice(0, 128)).astype(f32)
        west = jnp.where(here, pltpu.roll(first, 16 * t, 1) if t else first, west)
        last = pick(slice(0, 32), slice(COLS - 128, COLS)).astype(f32)
        turn = (16 * t + 16) % 128
        east = jnp.where(here, pltpu.roll(last, turn, 1) if turn else last, east)
        extra = pick(slice(32, 48), slice(0, 128)).astype(f32)
        extra = pltpu.roll(extra, 16 * t, 1) if t else extra
        bands = jnp.where(here[:8], extra[0:8], bands)
        seeds = jnp.where(here[:8], extra[8:16], seeds)
    blank = jnp.zeros((8, 128), f32)
    tail = jnp.concatenate([seeds, blank], axis=0).astype(bf16)
    for ref, value in ((west_ref, west), (east_ref, east)):
        ref[0:32, :] = value.astype(bf16)
        ref[96:112, :] = tail
    lane = iota((64, 128), 1)
    for ref, cols, shift in ((west_ref, slice(0, 128), 0), (east_ref, slice(COLS - 128, COLS), 8)):
        total = jnp.zeros((64, 128), f32)
        for g in range(16):
            parts = []
            for ch in (2 * g, 2 * g + 1):
                parts.append(up_ref[ch, :, cols].astype(f32))
                parts.append(cot_ref[ch, :, cols].astype(f32))
                parts.append(down_ref[ch, :, cols].astype(f32))
            whole = jnp.concatenate(parts, axis=0)
            turn = (8 * g + shift) % 128
            whole = pltpu.roll(whole, turn, 1) if turn else whole
            total = jnp.where(jnp.logical_and(lane >= 8 * g, lane < 8 * g + 8), whole, total)
        ref[32:96, :] = total.astype(bf16)
    chunk = jnp.concatenate([bands, blank], axis=0).astype(bf16)
    bands_ref[...] = jnp.broadcast_to(chunk[None], (32, 16, 128))


def main_kernel(
    place,
    feats_ref,
    bands_ref,
    own_ref,
    right_ref,
    left_ref,
    wr_ref,
    wc_ref,
    w1_ref,
    w2_ref,
    cot_ref,
    cot_up_ref,
    cot_down_ref,
    out_ref,
    send_ref,
    t1,
    t2,
    t2m,
    pv,
    hv,
    gv,
    g1,
    d1,
    acc,
    first_out,
    row_all,
    row3,
    qv,
    keep_rows,
    seed_rows,
    base_ref,
    keep_ref,
    cot_halo,
    every,
):
    s1 = place[0]
    s2 = place[1]
    r = lax.axis_index("row")
    c = lax.axis_index("col")
    turn = r // 2

    spread = (iota((K, BLK), 1) // 8 == iota((K, BLK), 0)).astype(f32).astype(bf16)
    sub = iota((8, BLK), 0)
    far = iota((8, BLK), 1) % 8 - sub

    def hits(s, half):
        return [far + 8 * half == 4 + (a - 1) * s for a in range(3)]

    def build(target, weight, s, mirrored):
        masks = [hits(s, half) for half in range(2)]
        for b in range(3):
            grown = []
            for a in range(3):
                if mirrored:
                    grown.append(dot_tn(weight[(2 - a) * 3 + (2 - b)], spread))
                else:
                    grown.append(dot(weight[a * 3 + b], spread))
            for half in range(2):
                m = masks[half]
                whole = jnp.zeros((K, 8, BLK), f32)
                for a in range(3):
                    whole = jnp.where(
                        jnp.broadcast_to(m[a][None], (K, 8, BLK)),
                        jnp.broadcast_to(grown[a][:, None, :], (K, 8, BLK)),
                        whole,
                    )
                at = (half * 3 + b) * BLK
                target[:, at : at + BLK] = whole.reshape(BLK, BLK).astype(bf16)

    build(t1, w1_ref, s1, False)
    build(t2, w2_ref, s2, False)
    build(t2m, w2_ref, s2, True)

    lane = iota((K, 128), 1)
    right = right_ref[0:32, :].astype(f32)
    left = left_ref[0:32, :].astype(f32)
    for t in range(8):
        r_turn = (128 - 16 * t) % 128
        l_turn = (112 - 16 * t) % 128
        halo = jnp.where(
            lane < 64,
            pltpu.roll(right, r_turn, 1) if r_turn else right,
            pltpu.roll(left, l_turn, 1) if l_turn else left,
        ).astype(bf16)
        every[32 * t : 32 * t + 32, 0:COLS] = feats_ref[t]
        every[32 * t : 32 * t + 32, COLS:] = halo
    weight = pltpu.roll(wc_ref[...].astype(f32), lax.rem(256 - 64 * turn, 256), 1).astype(bf16)
    q = dot(weight, every[...])
    qv[...] = q

    bands = bands_ref[...].astype(f32)[:, 0:8, :].reshape(256, 128).astype(bf16)
    row_t = dot(wr_ref[...], bands)
    row_all[...] = row_t.T
    core = lax.rem(r, 2)
    lane128 = iota((1, 128), 1)
    row_t = pltpu.roll(row_t, lax.rem(128 - 16 * core, 128), 1)
    row_t = jnp.where(lane128 < 16, row_t, 0.0)

    lane = iota((1, WIDE), 1)
    for step in range(3):
        slot = lax.rem(core + step + 7, 8)
        row3[16 * step : 16 * step + 16, :] = row_all[
            pl.ds(pl.multiple_of(16 * slot, 16), 16), :
        ]
        sides = []
        for ref in (own_ref, right_ref, left_ref):
            piece = ref[96:112, :].astype(f32)[0:1]
            piece = pltpu.roll(piece, lax.rem(128 - 16 * slot, 128), 1)
            number = piece[:, 0:1] * 65536.0 + piece[:, 1:2] * 256.0 + piece[:, 2:3]
            sides.append((number, piece[:, 3:4]))
        row_ok = jnp.logical_and(r + step >= 1, r + step <= 8).astype(f32)
        right_ok = row_ok * (c < 31).astype(f32)
        left_ok = row_ok * (c > 0).astype(f32)
        keep = jnp.where(
            lane < COLS,
            sides[0][1] * row_ok,
            jnp.where(lane < 576, sides[1][1] * right_ok, sides[2][1] * left_ok),
        )
        seed = jnp.where(
            lane < COLS, sides[0][0], jnp.where(lane < 576, sides[1][0], sides[2][0])
        )
        seed_rows[step] = seed.astype(jnp.int32)
        keep_rows[step] = keep

    lane64 = iota((64, 128), 1)
    right = right_ref[32:96, :].astype(f32)
    left = left_ref[32:96, :].astype(f32)
    for g in range(16):
        r_turn = (128 - 8 * g) % 128
        l_turn = 120 - 8 * g
        cot_halo[64 * g : 64 * g + 64, :] = jnp.where(
            lane64 < 64,
            pltpu.roll(right, r_turn, 1) if r_turn else right,
            pltpu.roll(left, l_turn, 1) if l_turn else left,
        )

    column = iota((8, WIDE), 1)
    column = c * COLS + jnp.where(column < 576, column, column - WIDE)

    def prepare(first_row, layer):
        local = first_row + iota((8, WIDE), 0)
        seed = jnp.where(
            local < 0, seed_rows[0], jnp.where(local < ROWS, seed_rows[1], seed_rows[2])
        )
        keep = jnp.where(
            local < 0, keep_rows[0], jnp.where(local < ROWS, keep_rows[1], keep_rows[2])
        )
        base = seed * 1000003 + layer * 7919
        base = base ^ ((r * ROWS + local) * 19349663)
        base_ref[...] = base ^ (column * 83492791)
        keep_ref[...] = keep * keep_boost

    def factor_of(p):
        keep = keep_ref[...]
        base = base_ref[...]
        parts = [mixed(base ^ wrapped(ch * 73856093), keep) for ch in (2 * p, 2 * p + 1)]
        return jnp.concatenate(parts, axis=0)

    def store_shifted(target, block, p, values, s):
        values = values.astype(bf16)
        for b, moved in enumerate((behind(values, s), values, ahead(values, s))):
            at = pl.multiple_of(block * 3 * BLK + b * BLK + 16 * p, 16)
            target[pl.ds(at, 16), :] = moved

    def pair_block(k, carry):
        rows = row3[pl.ds(pl.multiple_of(8 * k, 8), 8), :]
        keep = keep_rows[k // 2]
        for p in range(K // 2):
            parts = []
            for ch in (2 * p, 2 * p + 1):
                parts.append(keep * (rows[:, ch : ch + 1] + qv[ch : ch + 1, :]))
            store_shifted(pv, k, p, jnp.concatenate(parts, axis=0), s1)
        return carry

    lax.fori_loop(0, 6, pair_block, 0)

    def convolve(k, weight, values, to):
        acc[to] = dot(weight[...], values[k * 3 * BLK : (k + 2) * 3 * BLK, :])

    def hidden_block(k, at_acc):
        prepare(8 * k - 12, 1)
        for p in range(K // 2):
            at = 16 * p
            value, slope = gelu_parts(acc[at_acc, at : at + 16, :])
            factor = factor_of(p)
            store_shifted(hv, k, p, factor * value, s2)
            if 1 <= k <= 3:
                d1[(k - 1) * BLK + at : (k - 1) * BLK + at + 16, :] = factor * slope

    def grad_block(k, at_acc):
        prepare(8 * k - 8, 2)
        for p in range(K // 2):
            at = 16 * p
            value, slope = gelu_parts(acc[at_acc, at : at + 16, :])
            factor = factor_of(p)
            if k == 0:
                cot = cot_up_ref[at : at + 16, :].astype(f32)
            elif k == 3:
                cot = cot_down_ref[at : at + 16, :].astype(f32)
            else:
                parts = []
                for ch in (2 * p, 2 * p + 1):
                    parts.append(cot_ref[ch].astype(f32)[8 * (k - 1) : 8 * k])
                cot = jnp.concatenate(parts, axis=0)
            halo = []
            for i in range(2):
                first = 64 * p + 32 * i + 8 * k
                halo.append(cot_halo[first : first + 8, :])
            cot = jnp.concatenate([cot, jnp.concatenate(halo, axis=0)], axis=1)
            store_shifted(gv, k, p, cot * factor * slope, s2)
            if k == 1:
                first_out[at : at + 16, :] = (factor * value)[:, :COLS]
            if k == 2:
                upper = first_out[at : at + 16, :]
                lower = (factor * value)[:, :COLS]
                for i in range(2):
                    both = jnp.concatenate(
                        [upper[8 * i : 8 * i + 8], lower[8 * i : 8 * i + 8]], axis=0
                    )
                    out_ref[2 * p + i] = both.astype(bf16)

    def back_block(k, at_acc):
        g1[k * BLK : (k + 1) * BLK, :] = (
            acc[at_acc] * d1[k * BLK : (k + 1) * BLK, :]
        ).astype(bf16)

    jobs = [(convolve, k, t1, pv, functools.partial(hidden_block, k)) for k in range(5)]
    jobs += [(convolve, k, t2, hv, functools.partial(grad_block, k)) for k in range(4)]
    jobs += [(convolve, k, t2m, gv, functools.partial(back_block, k)) for k in range(3)]
    for i, (start, k, weight, values, _) in enumerate(jobs):
        start(k, weight, values, i % 2)
        if i:
            jobs[i - 1][4]((i - 1) % 2)
    jobs[-1][4]((len(jobs) - 1) % 2)

    crossed = []
    for half in range(2):
        total = jnp.zeros((BLK, 3 * BLK), f32)
        for k in (1, 2):
            start = k * 3 * BLK + BLK
            grads = gv[start : start + BLK, 0:COLS]
            start = (k + half) * 3 * BLK
            total = total + dot_nt(grads, hv[start : start + 3 * BLK, 0:COLS])
        crossed.append(total)
    gather8 = (iota((3 * BLK, 96), 0) // 8 == iota((3 * BLK, 96), 1)).astype(f32)
    masks = [hits(s2, half) for half in range(2)]
    second_rows = []
    for a in range(3):
        found = jnp.zeros((K, 8, 3 * BLK), f32)
        for half in range(2):
            m = jnp.concatenate([masks[half][a].astype(f32)] * 3, axis=1)
            found = found + crossed[half].reshape(K, 8, 3 * BLK) * m[None]
        second_rows.append(dot(jnp.sum(found, axis=1), gather8, HIGH))
    second_total = jnp.concatenate(second_rows, axis=0)

    place_j = iota((WIDE, 384), 0)
    place_j = jnp.where(place_j < 576, place_j, place_j - WIDE)
    moved_j = place_j + (iota((WIDE, 384), 1) // 128 - 1) * s1
    window = jnp.logical_and(moved_j >= 0, moved_j < COLS).astype(f32).astype(bf16)
    by_row = dot(g1[...], window)
    which = iota((3 * BLK, 384), 0)
    which = which // BLK * 8 + which % 8
    by_row = jnp.where(iota((3 * BLK, 384), 1) % 128 == which, by_row, 0.0)
    same = (iota((K, 3 * BLK), 1) % BLK // 8 == iota((K, 3 * BLK), 0)).astype(f32)
    by_row = dot(same, by_row, HIGH)
    across = iota((96, 3 * BLK), 1)
    down = iota((96, 3 * BLK), 0)
    moved_i = across // BLK * 8 + across % 8 - 4 + (down // K - 1) * s1
    inside = jnp.logical_and(moved_i >= 0, moved_i < ROWS)
    inside = jnp.logical_and(inside, across % BLK // 8 == down % K)
    by_col = dot(inside.astype(f32).astype(bf16), g1[...])
    by_col = [ahead(by_col, s1), by_col, behind(by_col, s1)]

    keep_own = keep_rows[1][:, 0:1]

    col_sum = jnp.zeros((K, WIDE), f32)
    row_sum = jnp.zeros((K, 128), f32)
    first_cols = []
    row_taps = []
    for a in range(3):
        seen = jnp.zeros((K, 128), f32)
        for b in range(3):
            seen = seen + dot_tn(
                w1_ref[a * 3 + b].astype(f32), by_row[:, 128 * b : 128 * b + 128], HIGH
            )
        row_sum = row_sum + pltpu.roll(seen, 128 - (4 - (a - 1) * s1), 1)
    for b in range(3):
        flat = jnp.concatenate([w1_ref[a * 3 + b] for a in range(3)], axis=0).astype(f32)
        col_sum = col_sum + dot_tn(flat, by_col[b], HIGH)
        from_cols = dot_nt(by_col[b][:, :COLS], q[:, :COLS], HIGH)
        from_rows = []
        for a in range(3):
            moved = pltpu.roll(by_row[:, 128 * b : 128 * b + 128], 128 - (4 - (a - 1) * s1), 1)
            from_rows.append(dot_nt(moved, row_t, HIGH))
        first_cols.append(from_cols + jnp.concatenate(from_rows, axis=0))
    first_total = jnp.concatenate(first_cols, axis=1) * keep_own
    row_sum = jnp.where(lane128 < 16, row_sum * keep_own, 0.0)
    row_sum = pltpu.roll(row_sum, 16 * r, 1)

    col_sum = col_sum * keep_own
    for g in range(4):
        send_ref[32 * g : 32 * g + 32, :] = col_sum[:, 128 * g : 128 * g + 128].astype(bf16)
    send_ref[128:224, :] = jnp.concatenate([first_total, second_total[:, 0:32]], axis=1).astype(bf16)
    send_ref[224:272, :] = jnp.concatenate(
        [second_total[0:48, 32:96], second_total[48:96, 32:96]], axis=1
    ).astype(bf16)
    send_ref[272:304, :] = row_sum.astype(bf16)


def four(own_ref, a_ref, b_ref, c_ref):
    pair = own_ref[...].astype(f32) + b_ref[...].astype(f32)
    return pair + (a_ref[...].astype(f32) + c_ref[...].astype(f32))


def middle_kernel(
    own_ref, a_ref, b_ref, c_ref, feats_ref, wc_ref, gcols_ref, send_ref
):
    r = lax.axis_index("row")
    total = four(own_ref, a_ref, b_ref, c_ref)
    weight = pltpu.roll(wc_ref[...].astype(f32), lax.rem(256 - 32 * r, 256), 1)[:, 0:K]
    grad_w = jnp.zeros((K, 256), f32)
    for g in range(4):
        part = total[32 * g : 32 * g + 32, :]
        gcols_ref[:, 128 * g : 128 * g + 128] = dot_tn(weight, part, HIGH).astype(bf16)
        seen = feats_ref[:, :, 128 * g : 128 * g + 128].reshape(256, 128)
        grad_w = grad_w + dot_nt(part, seen.astype(f32), HIGH)
    grad_w = pltpu.roll(grad_w, 64 * (r // 2), 1)
    send_ref[0:176, :] = total[128:304].astype(bf16)
    send_ref[176:208, :] = grad_w[:, 0:128].astype(bf16)
    send_ref[208:240, :] = grad_w[:, 128:256].astype(bf16)


def last_kernel(
    own_ref, a_ref, bands_ref, wr_ref, gband_ref, gwr_ref, gwc_ref, g1_ref, g2_ref
):
    r = lax.axis_index("row")
    c = lax.axis_index("col")
    total = own_ref[...].astype(f32) + a_ref[...].astype(f32)
    rest = jnp.concatenate([total[96:144, 0:64], total[96:144, 64:128]], axis=0)
    for a in range(3):
        for b in range(3):
            g1_ref[a * 3 + b] = total[32 * a : 32 * a + 32, 32 * b : 32 * b + 32]
        g2_ref[a * 3] = total[32 * a : 32 * a + 32, 96:128]
        g2_ref[a * 3 + 1] = rest[32 * a : 32 * a + 32, 0:32]
        g2_ref[a * 3 + 2] = rest[32 * a : 32 * a + 32, 32:64]
    rows = total[144:176, :]
    gwc_ref[:, 0:128] = total[176:208]
    gwc_ref[:, 128:256] = total[208:240]
    bands = bands_ref[...].astype(f32)[:, 0:8, :].reshape(256, 128)
    turned = pltpu.roll(rows, lax.rem(128 - 32 * (r // 2), 128), 1)
    gwr_ref[...] = dot_nt(turned, bands, HIGH)
    mine = pltpu.roll(wr_ref[...].astype(f32), lax.rem(256 - 8 * c, 256), 1)[:, 0:128]
    mine = dot_tn(mine, pltpu.roll(rows, lax.rem(128 - 16 * r, 128), 1), HIGH)
    gband_ref[...] = mine[0:8, 0:16].astype(bf16)


def call(kernel, shapes, args, scratch=(), scalars=0):
    whole = pl.BlockSpec(memory_space=pltpu.VMEM)
    return pl.pallas_call(
        kernel,
        out_shape=shapes,
        in_specs=[pl.BlockSpec(memory_space=pltpu.SMEM)] * scalars
        + [whole] * (len(args) - scalars),
        out_specs=jax.tree.map(lambda _: whole, shapes),
        scratch_shapes=list(scratch),
        compiler_params=pltpu.CompilerParams(vmem_limit_bytes=VMEM_LIMIT),
    )(*args)


def shape(dims, kind):
    return jax.ShapeDtypeStruct(dims, kind)


def per_device(
    band_emb,
    col_emb,
    w_row,
    w_col,
    first_kernel_weight,
    second_kernel_weight,
    cotangent,
    drop_seeds,
    tile_mask,
    dilations,
):
    rows = lax.axis_size("row")
    cols = lax.axis_size("col")

    south = [(i, (i + 1) % rows) for i in range(rows)]
    north = [(j, i) for i, j in south]
    cot_up = lax.ppermute(cotangent[:, 8:, :], "row", south)
    cot_down = lax.ppermute(cotangent[:, :8, :], "row", north)

    cols_t = col_emb.T
    own = call(
        first_kernel,
        shape((48, COLS), bf16),
        (drop_seeds, tile_mask, cols_t, band_emb.T),
        scalars=2,
    )
    beyond = [
        lax.ppermute(own, "row", [((i + 2 * s) % rows, i) for i in range(rows)]) for s in (1, 2, 3)
    ]
    flip = [(i, i ^ 1) for i in range(rows)]
    other = lax.ppermute(jnp.stack([own] + beyond), "row", flip)

    feats, west_edge, east_edge, bands = call(
        pack_kernel,
        (
            shape((8, K, COLS), bf16),
            shape((112, 128), bf16),
            shape((112, 128), bf16),
            shape((32, 16, 128), bf16),
        ),
        (own, *beyond, other, cotangent, cot_up, cot_down),
    )
    east = [(i, (i + 1) % cols) for i in range(cols)]
    west = [(j, i) for i, j in east]
    right = lax.ppermute(west_edge, "col", west)
    left = lax.ppermute(east_edge, "col", east)
    bands = lax.all_to_all(bands, "col", 0, 0)

    w1 = jnp.transpose(first_kernel_weight, (2, 3, 0, 1)).reshape(TAPS, K, K)
    w2 = jnp.transpose(second_kernel_weight, (2, 3, 0, 1)).reshape(TAPS, K, K)
    out_map, sums = call(
        main_kernel,
        (shape((K, ROWS, COLS), bf16), shape((304, 128), bf16)),
        (
            dilations,
            feats,
            bands,
            west_edge,
            right,
            left,
            w_row.T,
            w_col.T,
            w1,
            w2,
            cotangent,
            cot_up.reshape(BLK, COLS),
            cot_down.reshape(BLK, COLS),
        ),
        scratch=(
            pltpu.VMEM((BLK, 6 * BLK), bf16),
            pltpu.VMEM((BLK, 6 * BLK), bf16),
            pltpu.VMEM((BLK, 6 * BLK), bf16),
            pltpu.VMEM((18 * BLK, WIDE), bf16),
            pltpu.VMEM((15 * BLK, WIDE), bf16),
            pltpu.VMEM((12 * BLK, WIDE), bf16),
            pltpu.VMEM((3 * BLK, WIDE), bf16),
            pltpu.VMEM((3 * BLK, WIDE), f32),
            pltpu.VMEM((2, BLK, WIDE), f32),
            pltpu.VMEM((BLK, COLS), f32),
            pltpu.VMEM((128, K), f32),
            pltpu.VMEM((48, K), f32),
            pltpu.VMEM((K, WIDE), f32),
            pltpu.VMEM((3, 1, WIDE), f32),
            pltpu.VMEM((3, 1, WIDE), jnp.int32),
            pltpu.VMEM((8, WIDE), jnp.int32),
            pltpu.VMEM((8, WIDE), f32),
            pltpu.VMEM((32 * K, 128), f32),
            pltpu.VMEM((8 * K, WIDE), bf16),
        ),
        scalars=1,
    )

    def added(x, y):
        return (x.astype(f32) + y.astype(f32)).astype(bf16)

    def quarters(x, axis, count, place):
        step, size = place
        turned = lambda i, s: i - i // step % size * step + (i // step + s) % size * step
        return [
            lax.ppermute(x, axis, [(i, turned(i, s)) for i in range(count)]) for s in (1, 2, 3)
        ]

    sums = added(sums, lax.ppermute(sums, "row", flip))
    grad_cols, terms = call(
        middle_kernel,
        (shape((K, COLS), bf16), shape((240, 128), bf16)),
        (sums, *quarters(sums, "row", rows, (2, 4)), feats, w_col.T),
    )
    for place in ((1, 4), (4, 4)):
        one, two, three = quarters(terms, "col", cols, place)
        pair = terms.astype(f32) + two.astype(f32)
        terms = (pair + (one.astype(f32) + three.astype(f32))).astype(bf16)
    grad_band, grad_w_row, grad_w_col, grad_one, grad_two = call(
        last_kernel,
        (
            shape((8, ROWS), bf16),
            shape((K, 256), f32),
            shape((K, 256), f32),
            shape((TAPS, K, K), f32),
            shape((TAPS, K, K), f32),
        ),
        (
            terms,
            lax.ppermute(terms, "col", [(i, (i + 16) % cols) for i in range(cols)]),
            bands,
            w_row.T,
        ),
    )
    unfold = lambda x: jnp.transpose(x.reshape(3, 3, K, K), (2, 3, 0, 1))
    return (
        out_map,
        grad_band.T,
        grad_cols.T,
        grad_w_row.T,
        grad_w_col.T,
        unfold(grad_one),
        unfold(grad_two),
    )


def solution(mesh):
    placed = (
        P("row", "col"),
        P("col", "row"),
        P(),
        P(),
        P(),
        P(),
        P(None, "row", "col"),
        P("row", "col"),
        P("row", "col"),
        P(),
    )
    return jax.shard_map(
        per_device,
        mesh=mesh,
        in_specs=placed,
        out_specs=(P(None, "row", "col"), P("row", "col"), P("col", "row"), P(), P(), P(), P()),
        check_vma=False,
    )
```

```python
import functools

import jax
import jax.numpy as jnp
from jax import lax
from jax.experimental import pallas as pl
from jax.experimental.pallas import tpu as pltpu
from jax.sharding import PartitionSpec as P

tanh_scale = 0.7978845608028654
cubic_term = 0.044715
keep_boost = 4.0 / 3.0
slope_cubic = 3.0 * tanh_scale * cubic_term

K = 32
ROWS = 16
COLS = 512
WIDE = 640
TAPS = 9
BLK = 8 * K
HIGH = lax.Precision.HIGHEST
f32 = jnp.float32
bf16 = jnp.bfloat16


def dot(a, b, precision=None):
    return lax.dot_general(
        a, b, (((1,), (0,)), ((), ())), precision=precision, preferred_element_type=f32
    )


def dot_nt(a, b, precision=None):
    return lax.dot_general(
        a, b, (((1,), (1,)), ((), ())), precision=precision, preferred_element_type=f32
    )


def dot_tn(a, b, precision=None):
    return lax.dot_general(
        a, b, (((0,), (0,)), ((), ())), precision=precision, preferred_element_type=f32
    )


def iota(shape, dim):
    return lax.broadcasted_iota(jnp.int32, shape, dim)


def ahead(x, s):
    lane = iota((x.shape[0], 128), 1)
    turned = [pltpu.roll(x[:, i : i + 128], 128 - s, 1) for i in range(0, x.shape[1], 128)]
    nxt = turned[1:] + turned[:1]
    return jnp.concatenate(
        [jnp.where(lane >= 128 - s, n, t) for t, n in zip(turned, nxt)], axis=1
    )


def behind(x, s):
    lane = iota((x.shape[0], 128), 1)
    turned = [pltpu.roll(x[:, i : i + 128], s, 1) for i in range(0, x.shape[1], 128)]
    prv = turned[-1:] + turned[:-1]
    return jnp.concatenate([jnp.where(lane < s, p, t) for t, p in zip(turned, prv)], axis=1)


def mixed(base, factor):
    h = base * 668265261
    h = h ^ lax.shift_right_logical(h, 15)
    h = h * 374761393
    h = h ^ lax.shift_right_logical(h, 13)
    return jnp.where((h & 3) != 0, factor, 0.0)


def wrapped(number):
    return (number + 2**31) % 2**32 - 2**31


def gelu_parts(v):
    v2 = v * v
    t = jnp.tanh(v * (tanh_scale + (tanh_scale * cubic_term) * v2))
    p = 0.5 + 0.5 * t
    value = v * p
    slope = p + value * (1.0 - t) * (tanh_scale + slope_cubic * v2)
    return value, slope


def first_kernel(seed_ref, mask_ref, cols_ref, band_ref, cot_ref, out_ref):
    out_ref[0:32, :] = cols_ref[...]
    lane = iota((8, 128), 1)
    seed = seed_ref[0, 0]
    bytes_of = [seed >> 16 & 255, seed >> 8 & 255, seed & 255, mask_ref[0, 0]]
    numbers = jnp.zeros((8, 128), jnp.int32)
    for i, value in enumerate(bytes_of):
        numbers = jnp.where(lane == i, value, numbers)
    band = jnp.concatenate([band_ref[...].astype(f32), jnp.zeros((8, 112), f32)], axis=1)
    out_ref[32:48, 0:128] = jnp.concatenate([band, numbers.astype(f32)], axis=0).astype(bf16)
    out_ref[32:48, 128:] = jnp.zeros((16, COLS - 128), bf16)
    lane = iota((16, 128), 1)
    for side, cols, shift in ((0, slice(0, 128), 0), (1, slice(COLS - 128, COLS), 8)):
        for half in range(2):
            total = jnp.zeros((16, 128), f32)
            for i in range(16):
                piece = cot_ref[16 * half + i, :, cols].astype(f32)
                turn = (8 * i + shift) % 128
                piece = pltpu.roll(piece, turn, 1) if turn else piece
                here = jnp.logical_and(lane >= 8 * i, lane < 8 * i + 8)
                total = jnp.where(here, piece, total)
            at = 256 * side + 128 * half
            out_ref[48:64, at : at + 128] = total.astype(bf16)


def pack_kernel(
    own_ref, one_ref, two_ref, three_ref, other_ref,
    feats_ref, west_ref, east_ref, bands_ref,
):
    even = lax.rem(lax.axis_index("row"), 2) == 0
    lane = iota((32, 128), 1)
    mine = [own_ref, one_ref, two_ref, three_ref]
    west = jnp.zeros((32, 128), f32)
    east = jnp.zeros((32, 128), f32)
    bands = jnp.zeros((8, 128), f32)
    seeds = jnp.zeros((8, 128), f32)
    edges = []
    for t in range(8):
        a = mine[t // 2]
        b = other_ref.at[t // 2]
        if t % 2 == 0:
            pick = lambda rows, cols: jnp.where(even, a[rows, cols], b[rows, cols])
        else:
            pick = lambda rows, cols: jnp.where(even, b[rows, cols], a[rows, cols])
        feats_ref[t] = pick(slice(0, 32), slice(0, COLS))
        here = jnp.logical_and(lane >= 16 * t, lane < 16 * t + 16)
        first = pick(slice(0, 32), slice(0, 128)).astype(f32)
        west = jnp.where(here, pltpu.roll(first, 16 * t, 1) if t else first, west)
        last = pick(slice(0, 32), slice(COLS - 128, COLS)).astype(f32)
        turn = (16 * t + 16) % 128
        east = jnp.where(here, pltpu.roll(last, turn, 1) if turn else last, east)
        edges.append(pick(slice(48, 64), slice(0, COLS)).astype(f32) if t in (0, 1, 2, 7) else None)
        extra = pick(slice(32, 48), slice(0, 128)).astype(f32)
        extra = pltpu.roll(extra, 16 * t, 1) if t else extra
        bands = jnp.where(here[:8], extra[0:8], bands)
        seeds = jnp.where(here[:8], extra[8:16], seeds)
    blank = jnp.zeros((8, 128), f32)
    tail = jnp.concatenate([seeds, blank], axis=0).astype(bf16)
    for ref, value in ((west_ref, west), (east_ref, east)):
        ref[0:32, :] = value.astype(bf16)
        ref[96:112, :] = tail
    around = [edges[7], edges[0], edges[1]], [edges[0], edges[1], edges[2]]
    three = [jnp.where(even, x, y) for x, y in zip(*around)]
    rows = jnp.concatenate([three[0][8:16], three[1], three[2][0:8]], axis=0).astype(bf16)
    for ref, at in ((west_ref, 0), (east_ref, 256)):
        ref[32:64, :] = rows[:, at : at + 128]
        ref[64:96, :] = rows[:, at + 128 : at + 256]
    chunk = jnp.concatenate([bands, blank], axis=0).astype(bf16)
    bands_ref[...] = jnp.broadcast_to(chunk[None], (32, 16, 128))


def main_kernel(
    place,
    feats_ref,
    bands_ref,
    own_ref,
    right_ref,
    left_ref,
    wr_ref,
    wc_ref,
    w1_ref,
    w2_ref,
    cot_ref,
    inner_ref,
    outer_ref,
    out_ref,
    send_ref,
    t1,
    t2,
    t2m,
    pv,
    hv,
    gv,
    g1,
    d1,
    acc,
    first_out,
    row_all,
    row3,
    qv,
    keep_rows,
    seed_rows,
    base_ref,
    keep_ref,
    cot_halo,
    every,
):
    s1 = place[0]
    s2 = place[1]
    r = lax.axis_index("row")
    c = lax.axis_index("col")
    turn = r // 2

    spread = (iota((K, BLK), 1) // 8 == iota((K, BLK), 0)).astype(f32).astype(bf16)
    sub = iota((8, BLK), 0)
    far = iota((8, BLK), 1) % 8 - sub

    def hits(s, half):
        return [far + 8 * half == 4 + (a - 1) * s for a in range(3)]

    def build(target, weight, s, mirrored):
        masks = [hits(s, half) for half in range(2)]
        for b in range(3):
            grown = []
            for a in range(3):
                if mirrored:
                    grown.append(dot_tn(weight[(2 - a) * 3 + (2 - b)], spread))
                else:
                    grown.append(dot(weight[a * 3 + b], spread))
            for half in range(2):
                m = masks[half]
                whole = jnp.zeros((K, 8, BLK), f32)
                for a in range(3):
                    whole = jnp.where(
                        jnp.broadcast_to(m[a][None], (K, 8, BLK)),
                        jnp.broadcast_to(grown[a][:, None, :], (K, 8, BLK)),
                        whole,
                    )
                at = (half * 3 + b) * BLK
                target[:, at : at + BLK] = whole.reshape(BLK, BLK).astype(bf16)

    build(t1, w1_ref, s1, False)
    build(t2, w2_ref, s2, False)
    build(t2m, w2_ref, s2, True)

    lane = iota((K, 128), 1)
    right = right_ref[0:32, :].astype(f32)
    left = left_ref[0:32, :].astype(f32)
    for t in range(8):
        r_turn = (128 - 16 * t) % 128
        l_turn = (112 - 16 * t) % 128
        halo = jnp.where(
            lane < 64,
            pltpu.roll(right, r_turn, 1) if r_turn else right,
            pltpu.roll(left, l_turn, 1) if l_turn else left,
        ).astype(bf16)
        every[32 * t : 32 * t + 32, 0:COLS] = feats_ref[t]
        every[32 * t : 32 * t + 32, COLS:] = halo
    weight = pltpu.roll(wc_ref[...].astype(f32), lax.rem(256 - 64 * turn, 256), 1).astype(bf16)
    q = dot(weight, every[...])
    qv[...] = q

    bands = bands_ref[...].astype(f32)[:, 0:8, :].reshape(256, 128).astype(bf16)
    row_t = dot(wr_ref[...], bands)
    row_all[...] = row_t.T
    core = lax.rem(r, 2)
    lane128 = iota((1, 128), 1)
    row_t = pltpu.roll(row_t, lax.rem(128 - 16 * core, 128), 1)
    row_t = jnp.where(lane128 < 16, row_t, 0.0)

    lane = iota((1, WIDE), 1)
    for step in range(3):
        slot = lax.rem(core + step + 7, 8)
        row3[16 * step : 16 * step + 16, :] = row_all[
            pl.ds(pl.multiple_of(16 * slot, 16), 16), :
        ]
        sides = []
        for ref in (own_ref, right_ref, left_ref):
            piece = ref[96:112, :].astype(f32)[0:1]
            piece = pltpu.roll(piece, lax.rem(128 - 16 * slot, 128), 1)
            number = piece[:, 0:1] * 65536.0 + piece[:, 1:2] * 256.0 + piece[:, 2:3]
            sides.append((number, piece[:, 3:4]))
        row_ok = jnp.logical_and(r + step >= 1, r + step <= 8).astype(f32)
        right_ok = row_ok * (c < 31).astype(f32)
        left_ok = row_ok * (c > 0).astype(f32)
        keep = jnp.where(
            lane < COLS,
            sides[0][1] * row_ok,
            jnp.where(lane < 576, sides[1][1] * right_ok, sides[2][1] * left_ok),
        )
        seed = jnp.where(
            lane < COLS, sides[0][0], jnp.where(lane < 576, sides[1][0], sides[2][0])
        )
        seed_rows[step] = seed.astype(jnp.int32)
        keep_rows[step] = keep

    lane32 = iota((32, 128), 1)
    for ch in range(K):
        first = 32 + ch // 16 * 32
        right = right_ref[first : first + 32, :].astype(f32)
        left = left_ref[first : first + 32, :].astype(f32)
        r_turn = (128 - 8 * ch) % 128
        l_turn = (120 - 8 * ch) % 128
        cot_halo[32 * ch : 32 * ch + 32, :] = jnp.where(
            lane32 < 64,
            pltpu.roll(right, r_turn, 1) if r_turn else right,
            pltpu.roll(left, l_turn, 1) if l_turn else left,
        )

    column = iota((8, WIDE), 1)
    column = c * COLS + jnp.where(column < 576, column, column - WIDE)

    def prepare(first_row, layer):
        local = first_row + iota((8, WIDE), 0)
        seed = jnp.where(
            local < 0, seed_rows[0], jnp.where(local < ROWS, seed_rows[1], seed_rows[2])
        )
        keep = jnp.where(
            local < 0, keep_rows[0], jnp.where(local < ROWS, keep_rows[1], keep_rows[2])
        )
        base = seed * 1000003 + layer * 7919
        base = base ^ ((r * ROWS + local) * 19349663)
        base_ref[...] = base ^ (column * 83492791)
        keep_ref[...] = keep * keep_boost

    def factor_of(p):
        keep = keep_ref[...]
        base = base_ref[...]
        parts = [mixed(base ^ wrapped(ch * 73856093), keep) for ch in (2 * p, 2 * p + 1)]
        return jnp.concatenate(parts, axis=0)

    def store_shifted(target, block, p, values, s):
        values = values.astype(bf16)
        for b, moved in enumerate((behind(values, s), values, ahead(values, s))):
            at = pl.multiple_of(block * 3 * BLK + b * BLK + 16 * p, 16)
            target[pl.ds(at, 16), :] = moved

    def pair_block(k, carry):
        rows = row3[pl.ds(pl.multiple_of(8 * k, 8), 8), :]
        keep = keep_rows[k // 2]
        for p in range(K // 2):
            parts = []
            for ch in (2 * p, 2 * p + 1):
                parts.append(keep * (rows[:, ch : ch + 1] + qv[ch : ch + 1, :]))
            store_shifted(pv, k, p, jnp.concatenate(parts, axis=0), s1)
        return carry

    lax.fori_loop(0, 6, pair_block, 0)

    def convolve(k, weight, values, to):
        acc[to] = dot(weight[...], values[k * 3 * BLK : (k + 2) * 3 * BLK, :])

    def hidden_block(k, at_acc):
        prepare(8 * k - 12, 1)
        for p in range(K // 2):
            at = 16 * p
            value, slope = gelu_parts(acc[at_acc, at : at + 16, :])
            factor = factor_of(p)
            store_shifted(hv, k, p, factor * value, s2)
            if 1 <= k <= 3:
                d1[(k - 1) * BLK + at : (k - 1) * BLK + at + 16, :] = factor * slope

    def grad_block(k, at_acc):
        prepare(8 * k - 8, 2)
        for p in range(K // 2):
            at = 16 * p
            value, slope = gelu_parts(acc[at_acc, at : at + 16, :])
            factor = factor_of(p)
            if k == 0:
                cot = jnp.where(core == 0, outer_ref[at : at + 16, :], inner_ref[at : at + 16, :])
                cot = cot.astype(f32)
            elif k == 3:
                cot = jnp.where(core == 0, inner_ref[at : at + 16, :], outer_ref[at : at + 16, :])
                cot = cot.astype(f32)
            else:
                parts = []
                for ch in (2 * p, 2 * p + 1):
                    parts.append(cot_ref[ch].astype(f32)[8 * (k - 1) : 8 * k])
                cot = jnp.concatenate(parts, axis=0)
            halo = []
            for i in range(2):
                first = 64 * p + 32 * i + 8 * k
                halo.append(cot_halo[first : first + 8, :])
            cot = jnp.concatenate([cot, jnp.concatenate(halo, axis=0)], axis=1)
            store_shifted(gv, k, p, cot * factor * slope, s2)
            if k == 1:
                first_out[at : at + 16, :] = (factor * value)[:, :COLS]
            if k == 2:
                upper = first_out[at : at + 16, :]
                lower = (factor * value)[:, :COLS]
                for i in range(2):
                    both = jnp.concatenate(
                        [upper[8 * i : 8 * i + 8], lower[8 * i : 8 * i + 8]], axis=0
                    )
                    out_ref[2 * p + i] = both.astype(bf16)

    def back_block(k, at_acc):
        g1[k * BLK : (k + 1) * BLK, :] = (
            acc[at_acc] * d1[k * BLK : (k + 1) * BLK, :]
        ).astype(bf16)

    jobs = [(convolve, k, t1, pv, functools.partial(hidden_block, k)) for k in range(5)]
    jobs += [(convolve, k, t2, hv, functools.partial(grad_block, k)) for k in range(4)]
    jobs += [(convolve, k, t2m, gv, functools.partial(back_block, k)) for k in range(3)]
    for i, (start, k, weight, values, _) in enumerate(jobs):
        start(k, weight, values, i % 2)
        if i:
            jobs[i - 1][4]((i - 1) % 2)
    jobs[-1][4]((len(jobs) - 1) % 2)

    crossed = []
    for half in range(2):
        total = jnp.zeros((BLK, 3 * BLK), f32)
        for k in (1, 2):
            start = k * 3 * BLK + BLK
            grads = gv[start : start + BLK, 0:COLS]
            start = (k + half) * 3 * BLK
            total = total + dot_nt(grads, hv[start : start + 3 * BLK, 0:COLS])
        crossed.append(total)
    gather8 = (iota((3 * BLK, 96), 0) // 8 == iota((3 * BLK, 96), 1)).astype(f32)
    masks = [hits(s2, half) for half in range(2)]
    second_rows = []
    for a in range(3):
        found = jnp.zeros((K, 8, 3 * BLK), f32)
        for half in range(2):
            m = jnp.concatenate([masks[half][a].astype(f32)] * 3, axis=1)
            found = found + crossed[half].reshape(K, 8, 3 * BLK) * m[None]
        second_rows.append(dot(jnp.sum(found, axis=1), gather8, HIGH))
    second_total = jnp.concatenate(second_rows, axis=0)

    place_j = iota((WIDE, 384), 0)
    place_j = jnp.where(place_j < 576, place_j, place_j - WIDE)
    moved_j = place_j + (iota((WIDE, 384), 1) // 128 - 1) * s1
    window = jnp.logical_and(moved_j >= 0, moved_j < COLS).astype(f32).astype(bf16)
    by_row = dot(g1[...], window)
    which = iota((3 * BLK, 384), 0)
    which = which // BLK * 8 + which % 8
    by_row = jnp.where(iota((3 * BLK, 384), 1) % 128 == which, by_row, 0.0)
    same = (iota((K, 3 * BLK), 1) % BLK // 8 == iota((K, 3 * BLK), 0)).astype(f32)
    by_row = dot(same, by_row, HIGH)
    across = iota((96, 3 * BLK), 1)
    down = iota((96, 3 * BLK), 0)
    moved_i = across // BLK * 8 + across % 8 - 4 + (down // K - 1) * s1
    inside = jnp.logical_and(moved_i >= 0, moved_i < ROWS)
    inside = jnp.logical_and(inside, across % BLK // 8 == down % K)
    by_col = dot(inside.astype(f32).astype(bf16), g1[...])
    by_col = [ahead(by_col, s1), by_col, behind(by_col, s1)]

    keep_own = keep_rows[1][:, 0:1]

    col_sum = jnp.zeros((K, WIDE), f32)
    row_sum = jnp.zeros((K, 128), f32)
    first_cols = []
    row_taps = []
    for a in range(3):
        seen = jnp.zeros((K, 128), f32)
        for b in range(3):
            seen = seen + dot_tn(
                w1_ref[a * 3 + b].astype(f32), by_row[:, 128 * b : 128 * b + 128], HIGH
            )
        row_sum = row_sum + pltpu.roll(seen, 128 - (4 - (a - 1) * s1), 1)
    for b in range(3):
        flat = jnp.concatenate([w1_ref[a * 3 + b] for a in range(3)], axis=0).astype(f32)
        col_sum = col_sum + dot_tn(flat, by_col[b], HIGH)
        from_cols = dot_nt(by_col[b][:, :COLS], q[:, :COLS], HIGH)
        from_rows = []
        for a in range(3):
            moved = pltpu.roll(by_row[:, 128 * b : 128 * b + 128], 128 - (4 - (a - 1) * s1), 1)
            from_rows.append(dot_nt(moved, row_t, HIGH))
        first_cols.append(from_cols + jnp.concatenate(from_rows, axis=0))
    first_total = jnp.concatenate(first_cols, axis=1) * keep_own
    row_sum = jnp.where(lane128 < 16, row_sum * keep_own, 0.0)
    row_sum = pltpu.roll(row_sum, 16 * r, 1)

    col_sum = col_sum * keep_own
    for g in range(4):
        send_ref[32 * g : 32 * g + 32, :] = col_sum[:, 128 * g : 128 * g + 128].astype(bf16)
    send_ref[128:224, :] = jnp.concatenate([first_total, second_total[:, 0:32]], axis=1).astype(bf16)
    send_ref[224:272, :] = jnp.concatenate(
        [second_total[0:48, 32:96], second_total[48:96, 32:96]], axis=1
    ).astype(bf16)
    send_ref[272:304, :] = row_sum.astype(bf16)


def four(own_ref, a_ref, b_ref, c_ref):
    pair = own_ref[...].astype(f32) + b_ref[...].astype(f32)
    return pair + (a_ref[...].astype(f32) + c_ref[...].astype(f32))


def middle_kernel(
    own_ref, a_ref, b_ref, c_ref, feats_ref, wc_ref, gcols_ref, send_ref
):
    r = lax.axis_index("row")
    total = four(own_ref, a_ref, b_ref, c_ref)
    weight = pltpu.roll(wc_ref[...].astype(f32), lax.rem(256 - 32 * r, 256), 1)[:, 0:K]
    grad_w = jnp.zeros((K, 256), f32)
    for g in range(4):
        part = total[32 * g : 32 * g + 32, :]
        gcols_ref[:, 128 * g : 128 * g + 128] = dot_tn(weight, part, HIGH).astype(bf16)
        seen = feats_ref[:, :, 128 * g : 128 * g + 128].reshape(256, 128)
        grad_w = grad_w + dot_nt(part, seen.astype(f32), HIGH)
    grad_w = pltpu.roll(grad_w, 64 * (r // 2), 1)
    send_ref[0:176, :] = total[128:304].astype(bf16)
    send_ref[176:208, :] = grad_w[:, 0:128].astype(bf16)
    send_ref[208:240, :] = grad_w[:, 128:256].astype(bf16)


def last_kernel(
    own_ref, a_ref, bands_ref, wr_ref, gband_ref, gwr_ref, gwc_ref, g1_ref, g2_ref
):
    r = lax.axis_index("row")
    c = lax.axis_index("col")
    total = own_ref[...].astype(f32) + a_ref[...].astype(f32)
    rest = jnp.concatenate([total[96:144, 0:64], total[96:144, 64:128]], axis=0)
    for a in range(3):
        for b in range(3):
            g1_ref[a * 3 + b] = total[32 * a : 32 * a + 32, 32 * b : 32 * b + 32]
        g2_ref[a * 3] = total[32 * a : 32 * a + 32, 96:128]
        g2_ref[a * 3 + 1] = rest[32 * a : 32 * a + 32, 0:32]
        g2_ref[a * 3 + 2] = rest[32 * a : 32 * a + 32, 32:64]
    rows = total[144:176, :]
    gwc_ref[:, 0:128] = total[176:208]
    gwc_ref[:, 128:256] = total[208:240]
    bands = bands_ref[...].astype(f32)[:, 0:8, :].reshape(256, 128)
    turned = pltpu.roll(rows, lax.rem(128 - 32 * (r // 2), 128), 1)
    gwr_ref[...] = dot_nt(turned, bands, HIGH)
    mine = pltpu.roll(wr_ref[...].astype(f32), lax.rem(256 - 8 * c, 256), 1)[:, 0:128]
    mine = dot_tn(mine, pltpu.roll(rows, lax.rem(128 - 16 * r, 128), 1), HIGH)
    gband_ref[...] = mine[0:8, 0:16].astype(bf16)


def call(kernel, shapes, args, scratch=(), scalars=0, limit=8):
    whole = pl.BlockSpec(memory_space=pltpu.VMEM)
    return pl.pallas_call(
        kernel,
        out_shape=shapes,
        in_specs=[pl.BlockSpec(memory_space=pltpu.SMEM)] * scalars
        + [whole] * (len(args) - scalars),
        out_specs=jax.tree.map(lambda _: whole, shapes),
        scratch_shapes=list(scratch),
        compiler_params=pltpu.CompilerParams(vmem_limit_bytes=limit * 1024 * 1024),
    )(*args)


def shape(dims, kind):
    return jax.ShapeDtypeStruct(dims, kind)


def per_device(
    band_emb,
    col_emb,
    w_row,
    w_col,
    first_kernel_weight,
    second_kernel_weight,
    cotangent,
    drop_seeds,
    tile_mask,
    dilations,
):
    rows = lax.axis_size("row")
    cols = lax.axis_size("col")

    cols_t = col_emb.T
    own = call(
        first_kernel,
        shape((64, COLS), bf16),
        (drop_seeds, tile_mask, cols_t, band_emb.T, cotangent),
        scalars=2,
    )
    beyond = [
        lax.ppermute(own, "row", [((i + 2 * s) % rows, i) for i in range(rows)]) for s in (1, 2, 3)
    ]
    flip = [(i, i ^ 1) for i in range(rows)]
    other = lax.ppermute(jnp.stack([own] + beyond), "row", flip)

    feats, west_edge, east_edge, bands = call(
        pack_kernel,
        (
            shape((8, K, COLS), bf16),
            shape((112, 128), bf16),
            shape((112, 128), bf16),
            shape((32, 16, 128), bf16),
        ),
        (own, *beyond, other),
    )
    east = [(i, (i + 1) % cols) for i in range(cols)]
    west = [(j, i) for i, j in east]
    right = lax.ppermute(west_edge, "col", west)
    left = lax.ppermute(east_edge, "col", east)
    bands = lax.all_to_all(bands, "col", 0, 0)

    core = lax.rem(lax.axis_index("row"), 2)
    inner = lax.dynamic_slice_in_dim(cotangent, 8 * (1 - core), 8, 1)
    outer = lax.dynamic_slice_in_dim(cotangent, 8 * core, 8, 1)
    pairs = [(i, (i + 1 if i % 2 else i - 1) % rows) for i in range(rows)]
    inner = lax.ppermute(inner, "row", flip).reshape(BLK, COLS)
    outer = lax.ppermute(outer, "row", pairs).reshape(BLK, COLS)

    w1 = jnp.transpose(first_kernel_weight, (2, 3, 0, 1)).reshape(TAPS, K, K)
    w2 = jnp.transpose(second_kernel_weight, (2, 3, 0, 1)).reshape(TAPS, K, K)
    out_map, sums = call(
        main_kernel,
        (shape((K, ROWS, COLS), bf16), shape((304, 128), bf16)),
        (
            dilations,
            feats,
            bands,
            west_edge,
            right,
            left,
            w_row.T,
            w_col.T,
            w1,
            w2,
            cotangent,
            inner,
            outer,
        ),
        scratch=(
            pltpu.VMEM((BLK, 6 * BLK), bf16),
            pltpu.VMEM((BLK, 6 * BLK), bf16),
            pltpu.VMEM((BLK, 6 * BLK), bf16),
            pltpu.VMEM((18 * BLK, WIDE), bf16),
            pltpu.VMEM((15 * BLK, WIDE), bf16),
            pltpu.VMEM((12 * BLK, WIDE), bf16),
            pltpu.VMEM((3 * BLK, WIDE), bf16),
            pltpu.VMEM((3 * BLK, WIDE), f32),
            pltpu.VMEM((2, BLK, WIDE), f32),
            pltpu.VMEM((BLK, COLS), f32),
            pltpu.VMEM((128, K), f32),
            pltpu.VMEM((48, K), f32),
            pltpu.VMEM((K, WIDE), f32),
            pltpu.VMEM((3, 1, WIDE), f32),
            pltpu.VMEM((3, 1, WIDE), jnp.int32),
            pltpu.VMEM((8, WIDE), jnp.int32),
            pltpu.VMEM((8, WIDE), f32),
            pltpu.VMEM((32 * K, 128), f32),
            pltpu.VMEM((8 * K, WIDE), bf16),
        ),
        scalars=1,
        limit=44,
    )

    def added(x, y):
        return (x.astype(f32) + y.astype(f32)).astype(bf16)

    def quarters(x, axis, count, place):
        step, size = place
        turned = lambda i, s: i - i // step % size * step + (i // step + s) % size * step
        return [
            lax.ppermute(x, axis, [(i, turned(i, s)) for i in range(count)]) for s in (1, 2, 3)
        ]

    sums = added(sums, lax.ppermute(sums, "row", flip))
    grad_cols, terms = call(
        middle_kernel,
        (shape((K, COLS), bf16), shape((240, 128), bf16)),
        (sums, *quarters(sums, "row", rows, (2, 4)), feats, w_col.T),
    )
    for place in ((1, 4), (4, 4)):
        one, two, three = quarters(terms, "col", cols, place)
        pair = terms.astype(f32) + two.astype(f32)
        terms = (pair + (one.astype(f32) + three.astype(f32))).astype(bf16)
    grad_band, grad_w_row, grad_w_col, grad_one, grad_two = call(
        last_kernel,
        (
            shape((8, ROWS), bf16),
            shape((K, 256), f32),
            shape((K, 256), f32),
            shape((TAPS, K, K), f32),
            shape((TAPS, K, K), f32),
        ),
        (
            terms,
            lax.ppermute(terms, "col", [(i, (i + 16) % cols) for i in range(cols)]),
            bands,
            w_row.T,
        ),
    )
    unfold = lambda x: jnp.transpose(x.reshape(3, 3, K, K), (2, 3, 0, 1))
    return (
        out_map,
        grad_band.T,
        grad_cols.T,
        grad_w_row.T,
        grad_w_col.T,
        unfold(grad_one),
        unfold(grad_two),
    )


def solution(mesh):
    placed = (
        P("row", "col"),
        P("col", "row"),
        P(),
        P(),
        P(),
        P(),
        P(None, "row", "col"),
        P("row", "col"),
        P("row", "col"),
        P(),
    )
    return jax.shard_map(
        per_device,
        mesh=mesh,
        in_specs=placed,
        out_specs=(P(None, "row", "col"), P("row", "col"), P("col", "row"), P(), P(), P(), P()),
        check_vma=False,
    )
```

```python
import functools

import jax
import jax.numpy as jnp
from jax import lax
from jax.experimental import pallas as pl
from jax.experimental.pallas import tpu as pltpu
from jax.sharding import PartitionSpec as P

tanh_scale = 0.7978845608028654
cubic_term = 0.044715
keep_boost = 4.0 / 3.0
slope_cubic = 3.0 * tanh_scale * cubic_term

K = 32
ROWS = 16
COLS = 512
WIDE = 640
TAPS = 9
BLK = 8 * K
HIGH = lax.Precision.HIGHEST
f32 = jnp.float32
bf16 = jnp.bfloat16


def dot(a, b, precision=None):
    return lax.dot_general(
        a, b, (((1,), (0,)), ((), ())), precision=precision, preferred_element_type=f32
    )


def dot_nt(a, b, precision=None):
    return lax.dot_general(
        a, b, (((1,), (1,)), ((), ())), precision=precision, preferred_element_type=f32
    )


def dot_tn(a, b, precision=None):
    return lax.dot_general(
        a, b, (((0,), (0,)), ((), ())), precision=precision, preferred_element_type=f32
    )


def iota(shape, dim):
    return lax.broadcasted_iota(jnp.int32, shape, dim)


def ahead(x, s):
    lane = iota((x.shape[0], 128), 1)
    turned = [pltpu.roll(x[:, i : i + 128], 128 - s, 1) for i in range(0, x.shape[1], 128)]
    nxt = turned[1:] + turned[:1]
    return jnp.concatenate(
        [jnp.where(lane >= 128 - s, n, t) for t, n in zip(turned, nxt)], axis=1
    )


def behind(x, s):
    lane = iota((x.shape[0], 128), 1)
    turned = [pltpu.roll(x[:, i : i + 128], s, 1) for i in range(0, x.shape[1], 128)]
    prv = turned[-1:] + turned[:-1]
    return jnp.concatenate([jnp.where(lane < s, p, t) for t, p in zip(turned, prv)], axis=1)


def mixed(base, factor):
    h = base * 668265261
    h = h ^ lax.shift_right_logical(h, 15)
    h = h * 374761393
    h = h ^ lax.shift_right_logical(h, 13)
    return jnp.where((h & 3) != 0, factor, 0.0)


def wrapped(number):
    return (number + 2**31) % 2**32 - 2**31


def gelu_parts(v):
    v2 = v * v
    t = jnp.tanh(v * (tanh_scale + (tanh_scale * cubic_term) * v2))
    p = 0.5 + 0.5 * t
    value = v * p
    slope = p + value * (1.0 - t) * (tanh_scale + slope_cubic * v2)
    return value, slope


def first_kernel(seed_ref, mask_ref, cols_ref, band_ref, cot_ref, out_ref):
    out_ref[0:32, :] = cols_ref[...]
    lane = iota((8, 128), 1)
    seed = seed_ref[0, 0]
    bytes_of = [seed >> 16 & 255, seed >> 8 & 255, seed & 255, mask_ref[0, 0]]
    numbers = jnp.zeros((8, 128), jnp.int32)
    for i, value in enumerate(bytes_of):
        numbers = jnp.where(lane == i, value, numbers)
    band = jnp.concatenate([band_ref[...].astype(f32), jnp.zeros((8, 112), f32)], axis=1)
    out_ref[32:48, 0:128] = jnp.concatenate([band, numbers.astype(f32)], axis=0).astype(bf16)
    out_ref[32:48, 128:] = jnp.zeros((16, COLS - 128), bf16)
    lane = iota((16, 128), 1)
    for side, cols, shift in ((0, slice(0, 128), 0), (1, slice(COLS - 128, COLS), 8)):
        for half in range(2):
            total = jnp.zeros((16, 128), f32)
            for i in range(16):
                piece = cot_ref[16 * half + i, :, cols].astype(f32)
                turn = (8 * i + shift) % 128
                piece = pltpu.roll(piece, turn, 1) if turn else piece
                here = jnp.logical_and(lane >= 8 * i, lane < 8 * i + 8)
                total = jnp.where(here, piece, total)
            at = 256 * side + 128 * half
            out_ref[48:64, at : at + 128] = total.astype(bf16)


def pack_kernel(
    own_ref, one_ref, two_ref, three_ref, other_ref,
    feats_ref, west_ref, east_ref, bands_ref,
):
    even = lax.rem(lax.axis_index("row"), 2) == 0
    lane = iota((32, 128), 1)
    mine = [own_ref, one_ref, two_ref, three_ref]
    west = jnp.zeros((32, 128), f32)
    east = jnp.zeros((32, 128), f32)
    bands = jnp.zeros((8, 128), f32)
    seeds = jnp.zeros((8, 128), f32)
    edges = []
    for t in range(8):
        a = mine[t // 2]
        b = other_ref.at[t // 2]
        if t % 2 == 0:
            pick = lambda rows, cols: jnp.where(even, a[rows, cols], b[rows, cols])
        else:
            pick = lambda rows, cols: jnp.where(even, b[rows, cols], a[rows, cols])
        feats_ref[t] = pick(slice(0, 32), slice(0, COLS))
        here = jnp.logical_and(lane >= 16 * t, lane < 16 * t + 16)
        first = pick(slice(0, 32), slice(0, 128)).astype(f32)
        west = jnp.where(here, pltpu.roll(first, 16 * t, 1) if t else first, west)
        last = pick(slice(0, 32), slice(COLS - 128, COLS)).astype(f32)
        turn = (16 * t + 16) % 128
        east = jnp.where(here, pltpu.roll(last, turn, 1) if turn else last, east)
        edges.append(pick(slice(48, 64), slice(0, COLS)).astype(f32) if t in (0, 1, 2, 7) else None)
        extra = pick(slice(32, 48), slice(0, 128)).astype(f32)
        extra = pltpu.roll(extra, 16 * t, 1) if t else extra
        bands = jnp.where(here[:8], extra[0:8], bands)
        seeds = jnp.where(here[:8], extra[8:16], seeds)
    blank = jnp.zeros((8, 128), f32)
    tail = jnp.concatenate([seeds, blank], axis=0).astype(bf16)
    for ref, value in ((west_ref, west), (east_ref, east)):
        ref[0:32, :] = value.astype(bf16)
        ref[96:112, :] = tail
    around = [edges[7], edges[0], edges[1]], [edges[0], edges[1], edges[2]]
    three = [jnp.where(even, x, y) for x, y in zip(*around)]
    rows = jnp.concatenate([three[0][8:16], three[1], three[2][0:8]], axis=0).astype(bf16)
    for ref, at in ((west_ref, 0), (east_ref, 256)):
        ref[32:64, :] = rows[:, at : at + 128]
        ref[64:96, :] = rows[:, at + 128 : at + 256]
    chunk = jnp.concatenate([bands, blank], axis=0).astype(bf16)
    bands_ref[...] = jnp.broadcast_to(chunk[None], (32, 16, 128))


def main_kernel(
    place,
    feats_ref,
    bands_ref,
    own_ref,
    right_ref,
    left_ref,
    wr_ref,
    wc_ref,
    w1_ref,
    w2_ref,
    cot_ref,
    inner_ref,
    outer_ref,
    out_ref,
    send_ref,
    t1,
    t2,
    t2m,
    zv,
    gk,
    xv,
    hv,
    gv,
    g1,
    d1,
    acc,
    first_out,
    row_all,
    row3,
    keep_rows,
    seed_rows,
    base_ref,
    keep_ref,
    cot_halo,
    every,
):
    s1 = place[0]
    s2 = place[1]
    r = lax.axis_index("row")
    c = lax.axis_index("col")
    turn = r // 2

    spread = (iota((K, BLK), 1) // 8 == iota((K, BLK), 0)).astype(f32).astype(bf16)
    sub = iota((8, BLK), 0)
    far = iota((8, BLK), 1) % 8 - sub

    def hits(s, half):
        return [far + 8 * half == 4 + (a - 1) * s for a in range(3)]

    def build(target, weight, s, mirrored, by_tap=False):
        masks = [hits(s, half) for half in range(2)]
        for b in range(3):
            grown = []
            for a in range(3):
                if mirrored:
                    grown.append(dot_tn(weight[(2 - a) * 3 + (2 - b)], spread))
                else:
                    grown.append(dot(weight[a * 3 + b], spread))
            for half in range(2):
                m = masks[half]
                whole = jnp.zeros((K, 8, BLK), f32)
                for a in range(3):
                    whole = jnp.where(
                        jnp.broadcast_to(m[a][None], (K, 8, BLK)),
                        jnp.broadcast_to(grown[a][:, None, :], (K, 8, BLK)),
                        whole,
                    )
                at = (b * 2 + half if by_tap else half * 3 + b) * BLK
                target[:, at : at + BLK] = whole.reshape(BLK, BLK).astype(bf16)

    build(t1, w1_ref, s1, False, True)
    build(t2, w2_ref, s2, False)
    build(t2m, w2_ref, s2, True)

    lane = iota((K, 128), 1)
    right = right_ref[0:32, :].astype(f32)
    left = left_ref[0:32, :].astype(f32)
    for t in range(8):
        r_turn = (128 - 16 * t) % 128
        l_turn = (112 - 16 * t) % 128
        halo = jnp.where(
            lane < 64,
            pltpu.roll(right, r_turn, 1) if r_turn else right,
            pltpu.roll(left, l_turn, 1) if l_turn else left,
        ).astype(bf16)
        every[32 * t : 32 * t + 32, 0:COLS] = feats_ref[t]
        every[32 * t : 32 * t + 32, COLS:] = halo
    weight = pltpu.roll(wc_ref[...].astype(f32), lax.rem(256 - 64 * turn, 256), 1).astype(bf16)
    q = dot(weight, every[...])
    place_of = jnp.where(iota((1, WIDE), 1) < COLS, 0, jnp.where(iota((1, WIDE), 1) < 576, 1, 2))
    tile_of = [(place_of == m).astype(f32) for m in range(3)]
    ones = jnp.zeros((K, WIDE), f32)
    for m in range(3):
        row = iota((K, WIDE), 0)
        ones = jnp.where(jnp.logical_or(row == m, row == m + 3), tile_of[m], ones)
    q_rest = q - q.astype(bf16).astype(f32)
    for b, move in enumerate((behind, lambda x, s: x, ahead)):
        moved = move(q, s1)
        flags = move(ones, s1)
        for m in range(3):
            at = 128 * b + K * m
            xv[at : at + K, :] = (moved * flags[m : m + 1]).astype(bf16)
        xv[128 * b + 96 : 128 * b + 128, :] = flags.astype(bf16)
        xv[384 + K * b : 384 + K * b + K, :] = (move(q_rest, s1) * flags[0:1]).astype(bf16)
        xv[512 + K * b : 512 + K * b + K, :] = xv[128 * b : 128 * b + K, :]
    xv[480:512, :] = jnp.zeros((K, WIDE), bf16)
    xv[608:640, :] = jnp.zeros((K, WIDE), bf16)

    bands = bands_ref[...].astype(f32)[:, 0:8, :].reshape(256, 128).astype(bf16)
    row_t = dot(wr_ref[...], bands)
    row_all[...] = row_t.T
    core = lax.rem(r, 2)
    lane128 = iota((1, 128), 1)
    row_t = pltpu.roll(row_t, lax.rem(128 - 16 * core, 128), 1)
    row_t = jnp.where(lane128 < 16, row_t, 0.0)

    lane = iota((1, WIDE), 1)
    for step in range(3):
        slot = lax.rem(core + step + 7, 8)
        row3[16 * step : 16 * step + 16, :] = row_all[
            pl.ds(pl.multiple_of(16 * slot, 16), 16), :
        ]
        sides = []
        for ref in (own_ref, right_ref, left_ref):
            piece = ref[96:112, :].astype(f32)[0:1]
            piece = pltpu.roll(piece, lax.rem(128 - 16 * slot, 128), 1)
            number = piece[:, 0:1] * 65536.0 + piece[:, 1:2] * 256.0 + piece[:, 2:3]
            sides.append((number, piece[:, 3:4]))
        row_ok = jnp.logical_and(r + step >= 1, r + step <= 8).astype(f32)
        right_ok = row_ok * (c < 31).astype(f32)
        left_ok = row_ok * (c > 0).astype(f32)
        keep = jnp.where(
            lane < COLS,
            sides[0][1] * row_ok,
            jnp.where(lane < 576, sides[1][1] * right_ok, sides[2][1] * left_ok),
        )
        seed = jnp.where(
            lane < COLS, sides[0][0], jnp.where(lane < 576, sides[1][0], sides[2][0])
        )
        seed_rows[step] = seed.astype(jnp.int32)
        keep_rows[step] = keep

    lane32 = iota((32, 128), 1)
    for ch in range(K):
        first = 32 + ch // 16 * 32
        right = right_ref[first : first + 32, :].astype(f32)
        left = left_ref[first : first + 32, :].astype(f32)
        r_turn = (128 - 8 * ch) % 128
        l_turn = (120 - 8 * ch) % 128
        cot_halo[32 * ch : 32 * ch + 32, :] = jnp.where(
            lane32 < 64,
            pltpu.roll(right, r_turn, 1) if r_turn else right,
            pltpu.roll(left, l_turn, 1) if l_turn else left,
        )

    column = iota((8, WIDE), 1)
    column = c * COLS + jnp.where(column < 576, column, column - WIDE)

    def prepare(first_row, layer):
        local = first_row + iota((8, WIDE), 0)
        seed = jnp.where(
            local < 0, seed_rows[0], jnp.where(local < ROWS, seed_rows[1], seed_rows[2])
        )
        keep = jnp.where(
            local < 0, keep_rows[0], jnp.where(local < ROWS, keep_rows[1], keep_rows[2])
        )
        base = seed * 1000003 + layer * 7919
        base = base ^ ((r * ROWS + local) * 19349663)
        base_ref[...] = base ^ (column * 83492791)
        keep_ref[...] = keep * keep_boost

    def factor_of(p):
        keep = keep_ref[...]
        base = base_ref[...]
        parts = [mixed(base ^ wrapped(ch * 73856093), keep) for ch in (2 * p, 2 * p + 1)]
        return jnp.concatenate(parts, axis=0)

    def store_shifted(target, block, p, values, s):
        values = values.astype(bf16)
        for b, moved in enumerate((behind(values, s), values, ahead(values, s))):
            at = pl.multiple_of(block * 3 * BLK + b * BLK + 16 * p, 16)
            target[pl.ds(at, 16), :] = moved

    lane_m = jnp.where(lane128 < 96, lane128 // K, lane128 - 96)
    for k in range(6):
        rows = row3[8 * k : 8 * k + 8, :]
        keep = keep_rows[k // 2]
        keep = jnp.where(
            lane_m == 0,
            keep[:, 0:1],
            jnp.where(lane_m == 1, keep[:, COLS : COLS + 1], keep[:, WIDE - 1 : WIDE]),
        )
        keep = jnp.where(lane_m < 3, keep, 0.0)
        for p in range(K // 2):
            parts = []
            for ch in (2 * p, 2 * p + 1):
                picked = jnp.where(lane128 % K == ch, keep, 0.0)
                parts.append(jnp.where(lane128 < 96, picked, keep * rows[:, ch : ch + 1]))
            at = k * BLK + 16 * p
            zv[at : at + 16, :] = jnp.concatenate(parts, axis=0).astype(bf16)
    for k in (0, 2, 4):
        both = zv[k * BLK : (k + 2) * BLK, :]
        if k < 4:
            both = jnp.concatenate([both, zv[(k + 1) * BLK : (k + 3) * BLK, :]], axis=1)
        taps = [dot(t1[:, 2 * BLK * b : 2 * BLK * (b + 1)], both) for b in range(3)]
        for i in range(2 if k < 4 else 1):
            own_tile = jnp.zeros((BLK, 128), f32)
            for b in range(3):
                found = taps[b][:, 128 * i : 128 * i + 128]
                rest = found - found.astype(bf16).astype(f32)
                rest = jnp.where(jnp.logical_and(lane128 >= 99, lane128 < 102), pltpu.roll(rest, 3, 1), found)
                gk[k + i, :, 128 * b : 128 * b + 128] = rest.astype(bf16)
                here = jnp.logical_and(lane128 >= K * b, lane128 < K * b + K)
                own_tile = jnp.where(here, pltpu.roll(found, K * b, 1) if b else found, own_tile)
            rounded = own_tile.astype(bf16)
            gk[k + i, :, 384:512] = rounded
            gk[k + i, :, 512:640] = (own_tile - rounded.astype(f32)).astype(bf16)

    def convolve(k, weight, values, to):
        acc[to] = dot(weight[...], values[k * 3 * BLK : (k + 2) * 3 * BLK, :])

    def hidden_block(k, at_acc):
        prepare(8 * k - 12, 1)
        for p in range(K // 2):
            at = 16 * p
            value, slope = gelu_parts(acc[at_acc, at : at + 16, :])
            factor = factor_of(p)
            store_shifted(hv, k, p, factor * value, s2)
            if 1 <= k <= 3:
                d1[(k - 1) * BLK + at : (k - 1) * BLK + at + 16, :] = factor * slope

    def grad_block(k, at_acc):
        prepare(8 * k - 8, 2)
        for p in range(K // 2):
            at = 16 * p
            value, slope = gelu_parts(acc[at_acc, at : at + 16, :])
            factor = factor_of(p)
            if k == 0:
                cot = jnp.where(core == 0, outer_ref[at : at + 16, :], inner_ref[at : at + 16, :])
                cot = cot.astype(f32)
            elif k == 3:
                cot = jnp.where(core == 0, inner_ref[at : at + 16, :], outer_ref[at : at + 16, :])
                cot = cot.astype(f32)
            else:
                parts = []
                for ch in (2 * p, 2 * p + 1):
                    parts.append(cot_ref[ch].astype(f32)[8 * (k - 1) : 8 * k])
                cot = jnp.concatenate(parts, axis=0)
            halo = []
            for i in range(2):
                first = 64 * p + 32 * i + 8 * k
                halo.append(cot_halo[first : first + 8, :])
            cot = jnp.concatenate([cot, jnp.concatenate(halo, axis=0)], axis=1)
            store_shifted(gv, k, p, cot * factor * slope, s2)
            if k == 1:
                first_out[at : at + 16, :] = (factor * value)[:, :COLS]
            if k == 2:
                upper = first_out[at : at + 16, :]
                lower = (factor * value)[:, :COLS]
                for i in range(2):
                    both = jnp.concatenate(
                        [upper[8 * i : 8 * i + 8], lower[8 * i : 8 * i + 8]], axis=0
                    )
                    out_ref[2 * p + i] = both.astype(bf16)

    def back_block(k, at_acc):
        g1[k * BLK : (k + 1) * BLK, :] = (
            acc[at_acc] * d1[k * BLK : (k + 1) * BLK, :]
        ).astype(bf16)

    def convolve_first(k, weight, values, to):
        acc[to] = dot(weight[k], values[...])

    jobs = [(convolve_first, k, gk, xv, functools.partial(hidden_block, k)) for k in range(5)]
    jobs += [(convolve, k, t2, hv, functools.partial(grad_block, k)) for k in range(4)]
    jobs += [(convolve, k, t2m, gv, functools.partial(back_block, k)) for k in range(3)]
    for i, (start, k, weight, values, _) in enumerate(jobs):
        start(k, weight, values, i % 2)
        if i:
            jobs[i - 1][4]((i - 1) % 2)
    jobs[-1][4]((len(jobs) - 1) % 2)

    crossed = []
    for half in range(2):
        total = jnp.zeros((BLK, 3 * BLK), f32)
        for k in (1, 2):
            start = k * 3 * BLK + BLK
            grads = gv[start : start + BLK, 0:COLS]
            start = (k + half) * 3 * BLK
            total = total + dot_nt(grads, hv[start : start + 3 * BLK, 0:COLS])
        crossed.append(total)
    gather8 = (iota((3 * BLK, 96), 0) // 8 == iota((3 * BLK, 96), 1)).astype(f32)
    masks = [hits(s2, half) for half in range(2)]
    second_rows = []
    for a in range(3):
        found = jnp.zeros((K, 8, 3 * BLK), f32)
        for half in range(2):
            m = jnp.concatenate([masks[half][a].astype(f32)] * 3, axis=1)
            found = found + crossed[half].reshape(K, 8, 3 * BLK) * m[None]
        second_rows.append(dot(jnp.sum(found, axis=1), gather8, HIGH))
    second_total = jnp.concatenate(second_rows, axis=0)

    place_j = iota((WIDE, 384), 0)
    place_j = jnp.where(place_j < 576, place_j, place_j - WIDE)
    moved_j = place_j + (iota((WIDE, 384), 1) // 128 - 1) * s1
    window = jnp.logical_and(moved_j >= 0, moved_j < COLS).astype(f32).astype(bf16)
    by_row = dot(g1[...], window)
    which = iota((3 * BLK, 384), 0)
    which = which // BLK * 8 + which % 8
    by_row = jnp.where(iota((3 * BLK, 384), 1) % 128 == which, by_row, 0.0)
    same = (iota((K, 3 * BLK), 1) % BLK // 8 == iota((K, 3 * BLK), 0)).astype(f32)
    by_row = dot(same, by_row, HIGH)
    across = iota((96, 3 * BLK), 1)
    down = iota((96, 3 * BLK), 0)
    moved_i = across // BLK * 8 + across % 8 - 4 + (down // K - 1) * s1
    inside = jnp.logical_and(moved_i >= 0, moved_i < ROWS)
    inside = jnp.logical_and(inside, across % BLK // 8 == down % K)
    by_col = dot(inside.astype(f32).astype(bf16), g1[...])
    by_col = [ahead(by_col, s1), by_col, behind(by_col, s1)]

    keep_own = keep_rows[1][:, 0:1]

    col_sum = jnp.zeros((K, WIDE), f32)
    row_sum = jnp.zeros((K, 128), f32)
    first_cols = []
    row_taps = []
    for a in range(3):
        seen = jnp.zeros((K, 128), f32)
        for b in range(3):
            seen = seen + dot_tn(
                w1_ref[a * 3 + b].astype(f32), by_row[:, 128 * b : 128 * b + 128], HIGH
            )
        row_sum = row_sum + pltpu.roll(seen, 128 - (4 - (a - 1) * s1), 1)
    for b in range(3):
        flat = jnp.concatenate([w1_ref[a * 3 + b] for a in range(3)], axis=0).astype(f32)
        col_sum = col_sum + dot_tn(flat, by_col[b], HIGH)
        from_cols = dot_nt(by_col[b][:, :COLS], q[:, :COLS], HIGH)
        from_rows = []
        for a in range(3):
            moved = pltpu.roll(by_row[:, 128 * b : 128 * b + 128], 128 - (4 - (a - 1) * s1), 1)
            from_rows.append(dot_nt(moved, row_t, HIGH))
        first_cols.append(from_cols + jnp.concatenate(from_rows, axis=0))
    first_total = jnp.concatenate(first_cols, axis=1) * keep_own
    row_sum = jnp.where(lane128 < 16, row_sum * keep_own, 0.0)
    row_sum = pltpu.roll(row_sum, 16 * r, 1)

    col_sum = col_sum * keep_own
    for g in range(4):
        send_ref[32 * g : 32 * g + 32, :] = col_sum[:, 128 * g : 128 * g + 128].astype(bf16)
    send_ref[128:224, :] = jnp.concatenate([first_total, second_total[:, 0:32]], axis=1).astype(bf16)
    send_ref[224:272, :] = jnp.concatenate(
        [second_total[0:48, 32:96], second_total[48:96, 32:96]], axis=1
    ).astype(bf16)
    send_ref[272:304, :] = row_sum.astype(bf16)


def four(own_ref, a_ref, b_ref, c_ref):
    pair = own_ref[...].astype(f32) + b_ref[...].astype(f32)
    return pair + (a_ref[...].astype(f32) + c_ref[...].astype(f32))


def middle_kernel(
    own_ref, a_ref, b_ref, c_ref, feats_ref, wc_ref, gcols_ref, send_ref
):
    r = lax.axis_index("row")
    total = four(own_ref, a_ref, b_ref, c_ref)
    weight = pltpu.roll(wc_ref[...].astype(f32), lax.rem(256 - 32 * r, 256), 1)[:, 0:K]
    grad_w = jnp.zeros((K, 256), f32)
    for g in range(4):
        part = total[32 * g : 32 * g + 32, :]
        gcols_ref[:, 128 * g : 128 * g + 128] = dot_tn(weight, part, HIGH).astype(bf16)
        seen = feats_ref[:, :, 128 * g : 128 * g + 128].reshape(256, 128)
        grad_w = grad_w + dot_nt(part, seen.astype(f32), HIGH)
    grad_w = pltpu.roll(grad_w, 64 * (r // 2), 1)
    send_ref[0:176, :] = total[128:304].astype(bf16)
    send_ref[176:208, :] = grad_w[:, 0:128].astype(bf16)
    send_ref[208:240, :] = grad_w[:, 128:256].astype(bf16)


def last_kernel(
    own_ref, a_ref, bands_ref, wr_ref, gband_ref, gwr_ref, gwc_ref, g1_ref, g2_ref
):
    r = lax.axis_index("row")
    c = lax.axis_index("col")
    total = own_ref[...].astype(f32) + a_ref[...].astype(f32)
    rest = jnp.concatenate([total[96:144, 0:64], total[96:144, 64:128]], axis=0)
    for a in range(3):
        for b in range(3):
            g1_ref[a * 3 + b] = total[32 * a : 32 * a + 32, 32 * b : 32 * b + 32]
        g2_ref[a * 3] = total[32 * a : 32 * a + 32, 96:128]
        g2_ref[a * 3 + 1] = rest[32 * a : 32 * a + 32, 0:32]
        g2_ref[a * 3 + 2] = rest[32 * a : 32 * a + 32, 32:64]
    rows = total[144:176, :]
    gwc_ref[:, 0:128] = total[176:208]
    gwc_ref[:, 128:256] = total[208:240]
    bands = bands_ref[...].astype(f32)[:, 0:8, :].reshape(256, 128)
    turned = pltpu.roll(rows, lax.rem(128 - 32 * (r // 2), 128), 1)
    gwr_ref[...] = dot_nt(turned, bands, HIGH)
    mine = pltpu.roll(wr_ref[...].astype(f32), lax.rem(256 - 8 * c, 256), 1)[:, 0:128]
    mine = dot_tn(mine, pltpu.roll(rows, lax.rem(128 - 16 * r, 128), 1), HIGH)
    gband_ref[...] = mine[0:8, 0:16].astype(bf16)


def call(kernel, shapes, args, scratch=(), scalars=0, limit=8):
    whole = pl.BlockSpec(memory_space=pltpu.VMEM)
    return pl.pallas_call(
        kernel,
        out_shape=shapes,
        in_specs=[pl.BlockSpec(memory_space=pltpu.SMEM)] * scalars
        + [whole] * (len(args) - scalars),
        out_specs=jax.tree.map(lambda _: whole, shapes),
        scratch_shapes=list(scratch),
        compiler_params=pltpu.CompilerParams(vmem_limit_bytes=limit * 1024 * 1024),
    )(*args)


def shape(dims, kind):
    return jax.ShapeDtypeStruct(dims, kind)


def per_device(
    band_emb,
    col_emb,
    w_row,
    w_col,
    first_kernel_weight,
    second_kernel_weight,
    cotangent,
    drop_seeds,
    tile_mask,
    dilations,
):
    rows = lax.axis_size("row")
    cols = lax.axis_size("col")

    cols_t = col_emb.T
    own = call(
        first_kernel,
        shape((64, COLS), bf16),
        (drop_seeds, tile_mask, cols_t, band_emb.T, cotangent),
        scalars=2,
    )
    beyond = [
        lax.ppermute(own, "row", [((i + 2 * s) % rows, i) for i in range(rows)]) for s in (1, 2, 3)
    ]
    flip = [(i, i ^ 1) for i in range(rows)]
    other = lax.ppermute(jnp.stack([own] + beyond), "row", flip)

    feats, west_edge, east_edge, bands = call(
        pack_kernel,
        (
            shape((8, K, COLS), bf16),
            shape((112, 128), bf16),
            shape((112, 128), bf16),
            shape((32, 16, 128), bf16),
        ),
        (own, *beyond, other),
    )
    east = [(i, (i + 1) % cols) for i in range(cols)]
    west = [(j, i) for i, j in east]
    right = lax.ppermute(west_edge, "col", west)
    left = lax.ppermute(east_edge, "col", east)
    bands = lax.all_to_all(bands, "col", 0, 0)

    core = lax.rem(lax.axis_index("row"), 2)
    inner = lax.dynamic_slice_in_dim(cotangent, 8 * (1 - core), 8, 1)
    outer = lax.dynamic_slice_in_dim(cotangent, 8 * core, 8, 1)
    pairs = [(i, (i + 1 if i % 2 else i - 1) % rows) for i in range(rows)]
    inner = lax.ppermute(inner, "row", flip).reshape(BLK, COLS)
    outer = lax.ppermute(outer, "row", pairs).reshape(BLK, COLS)

    w1 = jnp.transpose(first_kernel_weight, (2, 3, 0, 1)).reshape(TAPS, K, K)
    w2 = jnp.transpose(second_kernel_weight, (2, 3, 0, 1)).reshape(TAPS, K, K)
    out_map, sums = call(
        main_kernel,
        (shape((K, ROWS, COLS), bf16), shape((304, 128), bf16)),
        (
            dilations,
            feats,
            bands,
            west_edge,
            right,
            left,
            w_row.T,
            w_col.T,
            w1,
            w2,
            cotangent,
            inner,
            outer,
        ),
        scratch=(
            pltpu.VMEM((BLK, 6 * BLK), bf16),
            pltpu.VMEM((BLK, 6 * BLK), bf16),
            pltpu.VMEM((BLK, 6 * BLK), bf16),
            pltpu.VMEM((6 * BLK, 128), bf16),
            pltpu.VMEM((5, BLK, 640), bf16),
            pltpu.VMEM((640, WIDE), bf16),
            pltpu.VMEM((15 * BLK, WIDE), bf16),
            pltpu.VMEM((12 * BLK, WIDE), bf16),
            pltpu.VMEM((3 * BLK, WIDE), bf16),
            pltpu.VMEM((3 * BLK, WIDE), f32),
            pltpu.VMEM((2, BLK, WIDE), f32),
            pltpu.VMEM((BLK, COLS), f32),
            pltpu.VMEM((128, K), f32),
            pltpu.VMEM((48, K), f32),
            pltpu.VMEM((3, 1, WIDE), f32),
            pltpu.VMEM((3, 1, WIDE), jnp.int32),
            pltpu.VMEM((8, WIDE), jnp.int32),
            pltpu.VMEM((8, WIDE), f32),
            pltpu.VMEM((32 * K, 128), f32),
            pltpu.VMEM((8 * K, WIDE), bf16),
        ),
        scalars=1,
        limit=44,
    )

    def added(x, y):
        return (x.astype(f32) + y.astype(f32)).astype(bf16)

    def quarters(x, axis, count, place):
        step, size = place
        turned = lambda i, s: i - i // step % size * step + (i // step + s) % size * step
        return [
            lax.ppermute(x, axis, [(i, turned(i, s)) for i in range(count)]) for s in (1, 2, 3)
        ]

    sums = added(sums, lax.ppermute(sums, "row", flip))
    grad_cols, terms = call(
        middle_kernel,
        (shape((K, COLS), bf16), shape((240, 128), bf16)),
        (sums, *quarters(sums, "row", rows, (2, 4)), feats, w_col.T),
    )
    for place in ((1, 4), (4, 4)):
        one, two, three = quarters(terms, "col", cols, place)
        pair = terms.astype(f32) + two.astype(f32)
        terms = (pair + (one.astype(f32) + three.astype(f32))).astype(bf16)
    grad_band, grad_w_row, grad_w_col, grad_one, grad_two = call(
        last_kernel,
        (
            shape((8, ROWS), bf16),
            shape((K, 256), f32),
            shape((K, 256), f32),
            shape((TAPS, K, K), f32),
            shape((TAPS, K, K), f32),
        ),
        (
            terms,
            lax.ppermute(terms, "col", [(i, (i + 16) % cols) for i in range(cols)]),
            bands,
            w_row.T,
        ),
    )
    unfold = lambda x: jnp.transpose(x.reshape(3, 3, K, K), (2, 3, 0, 1))
    return (
        out_map,
        grad_band.T,
        grad_cols.T,
        grad_w_row.T,
        grad_w_col.T,
        unfold(grad_one),
        unfold(grad_two),
    )


def solution(mesh):
    placed = (
        P("row", "col"),
        P("col", "row"),
        P(),
        P(),
        P(),
        P(),
        P(None, "row", "col"),
        P("row", "col"),
        P("row", "col"),
        P(),
    )
    return jax.shard_map(
        per_device,
        mesh=mesh,
        in_specs=placed,
        out_specs=(P(None, "row", "col"), P("row", "col"), P("col", "row"), P(), P(), P(), P()),
        check_vma=False,
    )
```

```python
import functools

import jax
import jax.numpy as jnp
from jax import lax
from jax.experimental import pallas as pl
from jax.experimental.pallas import tpu as pltpu
from jax.sharding import PartitionSpec as P

tanh_scale = 0.7978845608028654
cubic_term = 0.044715
keep_boost = 4.0 / 3.0
slope_cubic = 3.0 * tanh_scale * cubic_term

K = 32
ROWS = 16
COLS = 512
WIDE = 640
TAPS = 9
BLK = 8 * K
HIGH = lax.Precision.HIGHEST
f32 = jnp.float32
bf16 = jnp.bfloat16


def dot(a, b, precision=None):
    return lax.dot_general(
        a, b, (((1,), (0,)), ((), ())), precision=precision, preferred_element_type=f32
    )


def dot_nt(a, b, precision=None):
    return lax.dot_general(
        a, b, (((1,), (1,)), ((), ())), precision=precision, preferred_element_type=f32
    )


def dot_tn(a, b, precision=None):
    return lax.dot_general(
        a, b, (((0,), (0,)), ((), ())), precision=precision, preferred_element_type=f32
    )


def split(x):
    high = x.astype(bf16)
    return high, (x - high.astype(f32)).astype(bf16)


def fine(product, exact, x):
    high, low = split(x)
    return product(exact, high) + product(exact, low)


def fine_nt(a, b):
    a_high, a_low = split(a)
    b_high, b_low = split(b)
    return dot_nt(a_high, b_high) + (dot_nt(a_high, b_low) + dot_nt(a_low, b_high))


def iota(shape, dim):
    return lax.broadcasted_iota(jnp.int32, shape, dim)


def ahead(x, s):
    lane = iota((x.shape[0], 128), 1)
    turned = [pltpu.roll(x[:, i : i + 128], 128 - s, 1) for i in range(0, x.shape[1], 128)]
    nxt = turned[1:] + turned[:1]
    return jnp.concatenate(
        [jnp.where(lane >= 128 - s, n, t) for t, n in zip(turned, nxt)], axis=1
    )


def behind(x, s):
    lane = iota((x.shape[0], 128), 1)
    turned = [pltpu.roll(x[:, i : i + 128], s, 1) for i in range(0, x.shape[1], 128)]
    prv = turned[-1:] + turned[:-1]
    return jnp.concatenate([jnp.where(lane < s, p, t) for t, p in zip(turned, prv)], axis=1)


def mixed(base, factor):
    h = base * 668265261
    h = h ^ lax.shift_right_logical(h, 15)
    h = h * 374761393
    h = h ^ lax.shift_right_logical(h, 13)
    return jnp.where((h & 3) != 0, factor, 0.0)


def wrapped(number):
    return (number + 2**31) % 2**32 - 2**31


def gelu_parts(v):
    v2 = v * v
    t = jnp.tanh(v * (tanh_scale + (tanh_scale * cubic_term) * v2))
    p = 0.5 + 0.5 * t
    value = v * p
    slope = p + value * (1.0 - t) * (tanh_scale + slope_cubic * v2)
    return value, slope


def first_kernel(seed_ref, mask_ref, cols_ref, band_ref, cot_first_ref, cot_last_ref, out_ref):
    out_ref[0:32, :] = cols_ref[...]
    lane = iota((8, 128), 1)
    seed = seed_ref[0, 0]
    bytes_of = [seed >> 16 & 255, seed >> 8 & 255, seed & 255, mask_ref[0, 0]]
    numbers = jnp.zeros((8, 128), jnp.int32)
    for i, value in enumerate(bytes_of):
        numbers = jnp.where(lane == i, value, numbers)
    band = jnp.concatenate([band_ref[...].astype(f32), jnp.zeros((8, 112), f32)], axis=1)
    out_ref[32:48, 0:128] = jnp.concatenate([band, numbers.astype(f32)], axis=0).astype(bf16)
    out_ref[32:48, 128:] = jnp.zeros((16, COLS - 128), bf16)
    lane = iota((16, 128), 1)
    for side, cot_ref, shift in ((0, cot_first_ref, 0), (1, cot_last_ref, 8)):
        for half in range(2):
            total = jnp.zeros((16, 128), f32)
            for i in range(16):
                piece = cot_ref[16 * half + i].astype(f32)
                turn = (8 * i + shift) % 128
                piece = pltpu.roll(piece, turn, 1) if turn else piece
                here = jnp.logical_and(lane >= 8 * i, lane < 8 * i + 8)
                total = jnp.where(here, piece, total)
            at = 256 * side + 128 * half
            out_ref[48:64, at : at + 128] = total.astype(bf16)


def pack_kernel(
    own_ref, one_ref, two_ref, three_ref, other_ref,
    feats_ref, first_ref, second_ref, bands_ref,
):
    even = lax.rem(lax.axis_index("row"), 2) == 0
    lane = iota((32, 128), 1)
    mine = [own_ref, one_ref, two_ref, three_ref]
    west = jnp.zeros((32, 128), f32)
    east = jnp.zeros((32, 128), f32)
    bands = jnp.zeros((8, 128), f32)
    seeds = jnp.zeros((8, 128), f32)
    edges = []
    for t in range(8):
        a = mine[t // 2]
        b = other_ref.at[t // 2]
        if t % 2 == 0:
            pick = lambda rows, cols: jnp.where(even, a[rows, cols], b[rows, cols])
        else:
            pick = lambda rows, cols: jnp.where(even, b[rows, cols], a[rows, cols])
        feats_ref[t] = pick(slice(0, 32), slice(0, COLS))
        here = jnp.logical_and(lane >= 16 * t, lane < 16 * t + 16)
        first = pick(slice(0, 32), slice(0, 128)).astype(f32)
        west = jnp.where(here, pltpu.roll(first, 16 * t, 1) if t else first, west)
        last = pick(slice(0, 32), slice(COLS - 128, COLS)).astype(f32)
        turn = (16 * t + 16) % 128
        east = jnp.where(here, pltpu.roll(last, turn, 1) if turn else last, east)
        edges.append(pick(slice(48, 64), slice(0, COLS)).astype(f32) if t in (0, 1, 2, 7) else None)
        extra = pick(slice(32, 48), slice(0, 128)).astype(f32)
        extra = pltpu.roll(extra, 16 * t, 1) if t else extra
        bands = jnp.where(here[:8], extra[0:8], bands)
        seeds = jnp.where(here[:8], extra[8:16], seeds)
    blank = jnp.zeros((8, 128), f32)
    tail = jnp.concatenate([seeds, blank], axis=0).astype(bf16)
    around = [edges[7], edges[0], edges[1]], [edges[0], edges[1], edges[2]]
    three = [jnp.where(even, x, y) for x, y in zip(*around)]
    rows = jnp.concatenate([three[0][8:16], three[1], three[2][0:8]], axis=0).astype(bf16)
    whole = []
    for value, at in ((west, 0), (east, 256)):
        halves = [rows[:, at : at + 128], rows[:, at + 128 : at + 256]]
        whole.append(jnp.concatenate([value.astype(bf16)] + halves + [tail], axis=0))
    even_col = lax.rem(lax.axis_index("col"), 2) == 0
    first_ref[...] = jnp.where(even_col, whole[1], whole[0])
    second_ref[...] = jnp.where(even_col, whole[0], whole[1])
    chunk = jnp.concatenate([bands, blank], axis=0).astype(bf16)
    bands_ref[...] = jnp.broadcast_to(chunk[None], (32, 16, 128))


def main_kernel(
    place,
    feats_ref,
    bands_ref,
    own_ref,
    one_ref,
    two_ref,
    wr_ref,
    wc_ref,
    w1_ref,
    w2_ref,
    cot_ref,
    inner_ref,
    outer_ref,
    out_ref,
    send_ref,
    t1,
    t2,
    t2m,
    zv,
    gk,
    xv,
    hv,
    gv,
    g1,
    d1,
    acc,
    first_out,
    row_all,
    row3,
    keep_rows,
    seed_rows,
    base_ref,
    keep_ref,
    cot_halo,
    every,
):
    s1 = place[0]
    s2 = place[1]
    r = lax.axis_index("row")
    c = lax.axis_index("col")
    turn = r // 2
    even_col = lax.rem(c, 2) == 0
    right_all = jnp.where(even_col, one_ref[...], two_ref[...])
    left_all = jnp.where(even_col, two_ref[...], one_ref[...])

    spread = (iota((K, BLK), 1) // 8 == iota((K, BLK), 0)).astype(f32).astype(bf16)
    sub = iota((8, BLK), 0)
    far = iota((8, BLK), 1) % 8 - sub

    def hits(s, half):
        return [far + 8 * half == 4 + (a - 1) * s for a in range(3)]

    def build(target, weight, s, mirrored, by_tap=False):
        masks = [hits(s, half) for half in range(2)]
        for b in range(3):
            grown = []
            for a in range(3):
                if mirrored:
                    grown.append(dot_tn(weight[(2 - a) * 3 + (2 - b)], spread))
                else:
                    grown.append(dot(weight[a * 3 + b], spread))
            for half in range(2):
                m = masks[half]
                whole = jnp.zeros((K, 8, BLK), f32)
                for a in range(3):
                    whole = jnp.where(
                        jnp.broadcast_to(m[a][None], (K, 8, BLK)),
                        jnp.broadcast_to(grown[a][:, None, :], (K, 8, BLK)),
                        whole,
                    )
                at = (b * 2 + half if by_tap else half * 3 + b) * BLK
                target[:, at : at + BLK] = whole.reshape(BLK, BLK).astype(bf16)

    build(t1, w1_ref, s1, False, True)
    build(t2, w2_ref, s2, False)
    build(t2m, w2_ref, s2, True)

    lane = iota((K, 128), 1)
    right = right_all[0:32].astype(f32)
    left = left_all[0:32].astype(f32)
    for t in range(8):
        r_turn = (128 - 16 * t) % 128
        l_turn = (112 - 16 * t) % 128
        halo = jnp.where(
            lane < 64,
            pltpu.roll(right, r_turn, 1) if r_turn else right,
            pltpu.roll(left, l_turn, 1) if l_turn else left,
        ).astype(bf16)
        every[32 * t : 32 * t + 32, 0:COLS] = feats_ref[t]
        every[32 * t : 32 * t + 32, COLS:] = halo
    weight = pltpu.roll(wc_ref[...].astype(f32), lax.rem(256 - 64 * turn, 256), 1).astype(bf16)
    q = dot(weight, every[...])
    place_of = jnp.where(iota((1, WIDE), 1) < COLS, 0, jnp.where(iota((1, WIDE), 1) < 576, 1, 2))
    tile_of = [(place_of == m).astype(f32) for m in range(3)]
    ones = jnp.zeros((K, WIDE), f32)
    for m in range(3):
        row = iota((K, WIDE), 0)
        ones = jnp.where(jnp.logical_or(row == m, row == m + 3), tile_of[m], ones)
    q_rest = q - q.astype(bf16).astype(f32)
    for b, move in enumerate((behind, lambda x, s: x, ahead)):
        moved = move(q, s1)
        flags = move(ones, s1)
        for m in range(3):
            at = 128 * b + K * m
            xv[at : at + K, :] = (moved * flags[m : m + 1]).astype(bf16)
        xv[128 * b + 96 : 128 * b + 128, :] = flags.astype(bf16)
        xv[384 + K * b : 384 + K * b + K, :] = (move(q_rest, s1) * flags[0:1]).astype(bf16)
        xv[512 + K * b : 512 + K * b + K, :] = xv[128 * b : 128 * b + K, :]
    xv[480:512, :] = jnp.zeros((K, WIDE), bf16)
    xv[608:640, :] = jnp.zeros((K, WIDE), bf16)

    bands = bands_ref[...].astype(f32)[:, 0:8, :].reshape(256, 128).astype(bf16)
    row_t = dot(wr_ref[...], bands)
    row_all[...] = row_t.T
    core = lax.rem(r, 2)
    lane128 = iota((1, 128), 1)
    row_t = pltpu.roll(row_t, lax.rem(128 - 16 * core, 128), 1)
    row_t = jnp.where(lane128 < 16, row_t, 0.0)

    lane = iota((1, WIDE), 1)
    for step in range(3):
        slot = lax.rem(core + step + 7, 8)
        row3[16 * step : 16 * step + 16, :] = row_all[
            pl.ds(pl.multiple_of(16 * slot, 16), 16), :
        ]
        sides = []
        for edge in (own_ref[...], right_all, left_all):
            piece = edge[96:112].astype(f32)[0:1]
            piece = pltpu.roll(piece, lax.rem(128 - 16 * slot, 128), 1)
            number = piece[:, 0:1] * 65536.0 + piece[:, 1:2] * 256.0 + piece[:, 2:3]
            sides.append((number, piece[:, 3:4]))
        row_ok = jnp.logical_and(r + step >= 1, r + step <= 8).astype(f32)
        right_ok = row_ok * (c < 31).astype(f32)
        left_ok = row_ok * (c > 0).astype(f32)
        keep = jnp.where(
            lane < COLS,
            sides[0][1] * row_ok,
            jnp.where(lane < 576, sides[1][1] * right_ok, sides[2][1] * left_ok),
        )
        seed = jnp.where(
            lane < COLS, sides[0][0], jnp.where(lane < 576, sides[1][0], sides[2][0])
        )
        seed_rows[step] = seed.astype(jnp.int32)
        keep_rows[step] = keep

    lane32 = iota((32, 128), 1)
    for ch in range(K):
        first = 32 + ch // 16 * 32
        right = right_all[first : first + 32].astype(f32)
        left = left_all[first : first + 32].astype(f32)
        r_turn = (128 - 8 * ch) % 128
        l_turn = (120 - 8 * ch) % 128
        cot_halo[32 * ch : 32 * ch + 32, :] = jnp.where(
            lane32 < 64,
            pltpu.roll(right, r_turn, 1) if r_turn else right,
            pltpu.roll(left, l_turn, 1) if l_turn else left,
        )

    column = iota((8, WIDE), 1)
    column = c * COLS + jnp.where(column < 576, column, column - WIDE)

    def prepare(first_row, layer):
        local = first_row + iota((8, WIDE), 0)
        seed = jnp.where(
            local < 0, seed_rows[0], jnp.where(local < ROWS, seed_rows[1], seed_rows[2])
        )
        keep = jnp.where(
            local < 0, keep_rows[0], jnp.where(local < ROWS, keep_rows[1], keep_rows[2])
        )
        base = seed * 1000003 + layer * 7919
        base = base ^ ((r * ROWS + local) * 19349663)
        base_ref[...] = base ^ (column * 83492791)
        keep_ref[...] = keep * keep_boost

    def factor_of(p):
        keep = keep_ref[...]
        base = base_ref[...]
        parts = [mixed(base ^ wrapped(ch * 73856093), keep) for ch in (2 * p, 2 * p + 1)]
        return jnp.concatenate(parts, axis=0)

    def store_shifted(target, block, p, values, s):
        values = values.astype(bf16)
        for b, moved in enumerate((behind(values, s), values, ahead(values, s))):
            at = pl.multiple_of(block * 3 * BLK + b * BLK + 16 * p, 16)
            target[pl.ds(at, 16), :] = moved

    lane_m = jnp.where(lane128 < 96, lane128 // K, lane128 - 96)
    for k in range(6):
        rows = row3[8 * k : 8 * k + 8, :]
        keep = keep_rows[k // 2]
        keep = jnp.where(
            lane_m == 0,
            keep[:, 0:1],
            jnp.where(lane_m == 1, keep[:, COLS : COLS + 1], keep[:, WIDE - 1 : WIDE]),
        )
        keep = jnp.where(lane_m < 3, keep, 0.0)
        for p in range(K // 2):
            parts = []
            for ch in (2 * p, 2 * p + 1):
                picked = jnp.where(lane128 % K == ch, keep, 0.0)
                parts.append(jnp.where(lane128 < 96, picked, keep * rows[:, ch : ch + 1]))
            at = k * BLK + 16 * p
            zv[at : at + 16, :] = jnp.concatenate(parts, axis=0).astype(bf16)
    for k in (0, 2, 4):
        both = zv[k * BLK : (k + 2) * BLK, :]
        if k < 4:
            both = jnp.concatenate([both, zv[(k + 1) * BLK : (k + 3) * BLK, :]], axis=1)
        taps = [dot(t1[:, 2 * BLK * b : 2 * BLK * (b + 1)], both) for b in range(3)]
        for i in range(2 if k < 4 else 1):
            own_tile = jnp.zeros((BLK, 128), f32)
            for b in range(3):
                found = taps[b][:, 128 * i : 128 * i + 128]
                rest = found - found.astype(bf16).astype(f32)
                rest = jnp.where(jnp.logical_and(lane128 >= 99, lane128 < 102), pltpu.roll(rest, 3, 1), found)
                gk[k + i, :, 128 * b : 128 * b + 128] = rest.astype(bf16)
                here = jnp.logical_and(lane128 >= K * b, lane128 < K * b + K)
                own_tile = jnp.where(here, pltpu.roll(found, K * b, 1) if b else found, own_tile)
            rounded = own_tile.astype(bf16)
            gk[k + i, :, 384:512] = rounded
            gk[k + i, :, 512:640] = (own_tile - rounded.astype(f32)).astype(bf16)

    def convolve(k, weight, values, to):
        acc[to] = dot(weight[...], values[k * 3 * BLK : (k + 2) * 3 * BLK, :])

    def hidden_block(k, at_acc):
        prepare(8 * k - 12, 1)
        for p in range(K // 2):
            at = 16 * p
            value, slope = gelu_parts(acc[at_acc, at : at + 16, :])
            factor = factor_of(p)
            store_shifted(hv, k, p, factor * value, s2)
            if 1 <= k <= 3:
                d1[(k - 1) * BLK + at : (k - 1) * BLK + at + 16, :] = factor * slope

    def grad_block(k, at_acc):
        prepare(8 * k - 8, 2)
        for p in range(K // 2):
            at = 16 * p
            value, slope = gelu_parts(acc[at_acc, at : at + 16, :])
            factor = factor_of(p)
            if k == 0:
                cot = jnp.where(core == 0, outer_ref[at : at + 16, :], inner_ref[at : at + 16, :])
                cot = cot.astype(f32)
            elif k == 3:
                cot = jnp.where(core == 0, inner_ref[at : at + 16, :], outer_ref[at : at + 16, :])
                cot = cot.astype(f32)
            else:
                parts = []
                for ch in (2 * p, 2 * p + 1):
                    parts.append(cot_ref[ch].astype(f32)[8 * (k - 1) : 8 * k])
                cot = jnp.concatenate(parts, axis=0)
            halo = []
            for i in range(2):
                first = 64 * p + 32 * i + 8 * k
                halo.append(cot_halo[first : first + 8, :])
            cot = jnp.concatenate([cot, jnp.concatenate(halo, axis=0)], axis=1)
            store_shifted(gv, k, p, cot * factor * slope, s2)
            if k == 1:
                first_out[at : at + 16, :] = (factor * value)[:, :COLS]
            if k == 2:
                upper = first_out[at : at + 16, :]
                lower = (factor * value)[:, :COLS]
                for i in range(2):
                    both = jnp.concatenate(
                        [upper[8 * i : 8 * i + 8], lower[8 * i : 8 * i + 8]], axis=0
                    )
                    out_ref[2 * p + i] = both.astype(bf16)

    def back_block(k, at_acc):
        g1[k * BLK : (k + 1) * BLK, :] = (
            acc[at_acc] * d1[k * BLK : (k + 1) * BLK, :]
        ).astype(bf16)

    def convolve_first(k, weight, values, to):
        acc[to] = dot(weight[k], values[...])

    jobs = [(convolve_first, k, gk, xv, functools.partial(hidden_block, k)) for k in range(5)]
    jobs += [(convolve, k, t2, hv, functools.partial(grad_block, k)) for k in range(4)]
    jobs += [(convolve, k, t2m, gv, functools.partial(back_block, k)) for k in range(3)]
    for i, (start, k, weight, values, _) in enumerate(jobs):
        start(k, weight, values, i % 2)
        if i:
            jobs[i - 1][4]((i - 1) % 2)
    jobs[-1][4]((len(jobs) - 1) % 2)

    crossed = []
    for half in range(2):
        total = jnp.zeros((BLK, 3 * BLK), f32)
        for k in (1, 2):
            start = k * 3 * BLK + BLK
            grads = gv[start : start + BLK, 0:COLS]
            start = (k + half) * 3 * BLK
            total = total + dot_nt(grads, hv[start : start + 3 * BLK, 0:COLS])
        crossed.append(total)
    gather8 = (iota((3 * BLK, 96), 0) // 8 == iota((3 * BLK, 96), 1)).astype(f32).astype(bf16)
    offset = iota((8, 3 * BLK), 1) % 8 - iota((8, 3 * BLK), 0)
    folded = []
    for a in range(3):
        found = jnp.zeros((K, 8, 3 * BLK), f32)
        for half in range(2):
            m = offset + 8 * half == 4 + (a - 1) * s2
            found = jnp.where(
                jnp.broadcast_to(m[None], found.shape), crossed[half].reshape(found.shape), found
            )
        folded.append(jnp.sum(found, axis=1))
    folded = jnp.concatenate(folded, axis=0)
    second_total = fine(lambda e, x: dot(x, e), gather8, folded)

    place_j = iota((WIDE, 128), 0)
    place_j = jnp.where(place_j < 576, place_j, place_j - WIDE)
    which = iota((3 * BLK, 128), 0)
    which = iota((3 * BLK, 128), 1) == which // BLK * 8 + which % 8
    same = (iota((K, 3 * BLK), 1) % BLK // 8 == iota((K, 3 * BLK), 0)).astype(f32).astype(bf16)
    by_row = []
    for b in range(3):
        moved_j = place_j + (b - 1) * s1
        window = jnp.logical_and(moved_j >= 0, moved_j < COLS).astype(f32).astype(bf16)
        by_row.append(fine(dot, same, jnp.where(which, dot(g1[...], window), 0.0)))
    across = iota((96, 3 * BLK), 1)
    down = iota((96, 3 * BLK), 0)
    moved_i = across // BLK * 8 + across % 8 - 4 + (down // K - 1) * s1
    inside = jnp.logical_and(moved_i >= 0, moved_i < ROWS)
    inside = jnp.logical_and(inside, across % BLK // 8 == down % K)
    by_col = dot(inside.astype(f32).astype(bf16), g1[...])
    by_col = jnp.concatenate([ahead(by_col, s1), by_col, behind(by_col, s1)], axis=0)

    keep_own = keep_rows[1][:, 0:1]
    weights = [w1_ref[a * 3 + b] for b in range(3) for a in range(3)]
    col_sum = fine(dot_tn, jnp.concatenate(weights, axis=0), by_col)
    row_sum = jnp.zeros((K, 128), f32)
    turned = []
    for a in range(3):
        turns = 128 - (4 - (a - 1) * s1)
        flat = jnp.concatenate([w1_ref[a * 3 + b] for b in range(3)], axis=0)
        row_sum = row_sum + pltpu.roll(
            fine(dot_tn, flat, jnp.concatenate(by_row, axis=0)), turns, 1
        )
        turned.append([pltpu.roll(by_row[b], turns, 1) for b in range(3)])
    turned = jnp.concatenate([turned[a][b] for b in range(3) for a in range(3)], axis=0)
    first_all = fine_nt(by_col[:, :COLS], q[:, :COLS]) + fine_nt(turned, row_t)
    first_total = jnp.concatenate([first_all[96 * b : 96 * b + 96] for b in range(3)], axis=1)
    first_total = first_total * keep_own
    row_sum = jnp.where(lane128 < 16, row_sum * keep_own, 0.0)
    row_sum = pltpu.roll(row_sum, 16 * r, 1)

    col_sum = col_sum * keep_own
    for g in range(4):
        send_ref[32 * g : 32 * g + 32, :] = col_sum[:, 128 * g : 128 * g + 128].astype(bf16)
    send_ref[128:224, :] = jnp.concatenate([first_total, second_total[:, 0:32]], axis=1).astype(bf16)
    send_ref[224:272, :] = jnp.concatenate(
        [second_total[0:48, 32:96], second_total[48:96, 32:96]], axis=1
    ).astype(bf16)
    send_ref[272:304, :] = row_sum.astype(bf16)


def four(own_ref, a_ref, b_ref, c_ref):
    pair = own_ref[...].astype(f32) + b_ref[...].astype(f32)
    return pair + (a_ref[...].astype(f32) + c_ref[...].astype(f32))


def middle_kernel(
    own_ref, a_ref, b_ref, c_ref, feats_ref, wc_ref, gcols_ref, send_ref
):
    r = lax.axis_index("row")
    total = four(own_ref, a_ref, b_ref, c_ref)
    weight = pltpu.roll(wc_ref[...].astype(f32), lax.rem(256 - 32 * r, 256), 1)
    weight = weight[:, 0:K].astype(bf16)
    grad_w = jnp.zeros((K, 256), f32)
    for g in range(4):
        part = total[32 * g : 32 * g + 32, :]
        gcols_ref[:, 128 * g : 128 * g + 128] = fine(dot_tn, weight, part).astype(bf16)
        seen = feats_ref[:, :, 128 * g : 128 * g + 128].reshape(256, 128)
        grad_w = grad_w + fine(lambda e, x: dot_nt(x, e), seen, part)
    grad_w = pltpu.roll(grad_w, 64 * (r // 2), 1)
    send_ref[0:176, :] = total[128:304].astype(bf16)
    send_ref[176:208, :] = grad_w[:, 0:128].astype(bf16)
    send_ref[208:240, :] = grad_w[:, 128:256].astype(bf16)


def last_kernel(
    own_ref, a_ref, bands_ref, wr_ref, gband_ref, gwr_ref, gwc_ref, g1_ref, g2_ref
):
    r = lax.axis_index("row")
    c = lax.axis_index("col")
    total = own_ref[...].astype(f32) + a_ref[...].astype(f32)
    rest = jnp.concatenate([total[96:144, 0:64], total[96:144, 64:128]], axis=0)
    for a in range(3):
        for b in range(3):
            g1_ref[a * 3 + b] = total[32 * a : 32 * a + 32, 32 * b : 32 * b + 32]
        g2_ref[a * 3] = total[32 * a : 32 * a + 32, 96:128]
        g2_ref[a * 3 + 1] = rest[32 * a : 32 * a + 32, 0:32]
        g2_ref[a * 3 + 2] = rest[32 * a : 32 * a + 32, 32:64]
    rows = total[144:176, :]
    gwc_ref[:, 0:128] = total[176:208]
    gwc_ref[:, 128:256] = total[208:240]
    bands = bands_ref[...].astype(f32)[:, 0:8, :].reshape(256, 128)
    turned = pltpu.roll(rows, lax.rem(128 - 32 * (r // 2), 128), 1)
    gwr_ref[...] = fine(lambda e, x: dot_nt(x, e), bands.astype(bf16), turned)
    mine = pltpu.roll(wr_ref[...].astype(f32), lax.rem(256 - 8 * c, 256), 1)[:, 0:128]
    mine = fine(dot_tn, mine.astype(bf16), pltpu.roll(rows, lax.rem(128 - 16 * r, 128), 1))
    gband_ref[...] = mine[0:8, 0:16].astype(bf16)


def call(kernel, shapes, args, scratch=(), scalars=0, limit=8, blocks={}):
    whole = pl.BlockSpec(memory_space=pltpu.VMEM)
    specs = [pl.BlockSpec(memory_space=pltpu.SMEM)] * scalars
    specs += [whole] * (len(args) - scalars)
    for i, (dims, at) in blocks.items():
        specs[i] = pl.BlockSpec(dims, lambda _, at=at: at)
    return pl.pallas_call(
        kernel,
        out_shape=shapes,
        grid=(1,) if blocks else (),
        in_specs=specs,
        out_specs=jax.tree.map(lambda _: whole, shapes),
        scratch_shapes=list(scratch),
        compiler_params=pltpu.CompilerParams(vmem_limit_bytes=limit * 1024 * 1024),
    )(*args)


def shape(dims, kind):
    return jax.ShapeDtypeStruct(dims, kind)


def per_device(
    band_emb,
    col_emb,
    w_row,
    w_col,
    first_kernel_weight,
    second_kernel_weight,
    cotangent,
    drop_seeds,
    tile_mask,
    dilations,
):
    rows = lax.axis_size("row")
    cols = lax.axis_size("col")

    cols_t = col_emb.T
    own = call(
        first_kernel,
        shape((64, COLS), bf16),
        (drop_seeds, tile_mask, cols_t, band_emb.T, cotangent, cotangent),
        blocks={4: ((K, ROWS, 128), (0, 0, 0)), 5: ((K, ROWS, 128), (0, 0, COLS // 128 - 1))},
        scalars=2,
    )
    beyond = [
        lax.ppermute(own, "row", [((i + 2 * s) % rows, i) for i in range(rows)]) for s in (1, 2, 3)
    ]
    flip = [(i, i ^ 1) for i in range(rows)]
    other = lax.ppermute(jnp.stack([own] + beyond), "row", flip)

    feats, edge_first, edge_second, bands = call(
        pack_kernel,
        (
            shape((8, K, COLS), bf16),
            shape((112, 128), bf16),
            shape((112, 128), bf16),
            shape((32, 16, 128), bf16),
        ),
        (own, *beyond, other),
    )
    inside = [(i, i ^ 1) for i in range(cols)]
    between = [(i, (i + 1 if i % 2 else i - 1) % cols) for i in range(cols)]
    edge_one = lax.ppermute(edge_first, "col", inside)
    edge_two = lax.ppermute(edge_second, "col", between)
    bands = lax.all_to_all(bands, "col", 0, 0)

    core = lax.rem(lax.axis_index("row"), 2)
    inner = lax.dynamic_slice_in_dim(cotangent, 8 * (1 - core), 8, 1)
    outer = lax.dynamic_slice_in_dim(cotangent, 8 * core, 8, 1)
    pairs = [(i, (i + 1 if i % 2 else i - 1) % rows) for i in range(rows)]
    inner = lax.ppermute(inner, "row", flip).reshape(BLK, COLS)
    outer = lax.ppermute(outer, "row", pairs).reshape(BLK, COLS)

    w1 = jnp.transpose(first_kernel_weight, (2, 3, 0, 1)).reshape(TAPS, K, K)
    w2 = jnp.transpose(second_kernel_weight, (2, 3, 0, 1)).reshape(TAPS, K, K)
    out_map, sums = call(
        main_kernel,
        (shape((K, ROWS, COLS), bf16), shape((304, 128), bf16)),
        (
            dilations,
            feats,
            bands,
            edge_first,
            edge_one,
            edge_two,
            w_row.T,
            w_col.T,
            w1,
            w2,
            cotangent,
            inner,
            outer,
        ),
        scratch=(
            pltpu.VMEM((BLK, 6 * BLK), bf16),
            pltpu.VMEM((BLK, 6 * BLK), bf16),
            pltpu.VMEM((BLK, 6 * BLK), bf16),
            pltpu.VMEM((6 * BLK, 128), bf16),
            pltpu.VMEM((5, BLK, 640), bf16),
            pltpu.VMEM((640, WIDE), bf16),
            pltpu.VMEM((15 * BLK, WIDE), bf16),
            pltpu.VMEM((12 * BLK, WIDE), bf16),
            pltpu.VMEM((3 * BLK, WIDE), bf16),
            pltpu.VMEM((3 * BLK, WIDE), f32),
            pltpu.VMEM((2, BLK, WIDE), f32),
            pltpu.VMEM((BLK, COLS), f32),
            pltpu.VMEM((128, K), f32),
            pltpu.VMEM((48, K), f32),
            pltpu.VMEM((3, 1, WIDE), f32),
            pltpu.VMEM((3, 1, WIDE), jnp.int32),
            pltpu.VMEM((8, WIDE), jnp.int32),
            pltpu.VMEM((8, WIDE), f32),
            pltpu.VMEM((32 * K, 128), f32),
            pltpu.VMEM((8 * K, WIDE), bf16),
        ),
        scalars=1,
        limit=44,
    )

    def added(x, y):
        return (x.astype(f32) + y.astype(f32)).astype(bf16)

    def quarters(x, axis, count, place):
        step, size = place
        turned = lambda i, s: i - i // step % size * step + (i // step + s) % size * step
        return [
            lax.ppermute(x, axis, [(i, turned(i, s)) for i in range(count)]) for s in (1, 2, 3)
        ]

    sums = added(sums, lax.ppermute(sums, "row", flip))
    grad_cols, terms = call(
        middle_kernel,
        (shape((K, COLS), bf16), shape((240, 128), bf16)),
        (sums, *quarters(sums, "row", rows, (2, 4)), feats, w_col.T),
    )
    for place in ((1, 4), (4, 4)):
        one, two, three = quarters(terms, "col", cols, place)
        pair = terms.astype(f32) + two.astype(f32)
        terms = (pair + (one.astype(f32) + three.astype(f32))).astype(bf16)
    grad_band, grad_w_row, grad_w_col, grad_one, grad_two = call(
        last_kernel,
        (
            shape((8, ROWS), bf16),
            shape((K, 256), f32),
            shape((K, 256), f32),
            shape((TAPS, K, K), f32),
            shape((TAPS, K, K), f32),
        ),
        (
            terms,
            lax.ppermute(terms, "col", [(i, (i + 16) % cols) for i in range(cols)]),
            bands,
            w_row.T,
        ),
    )
    unfold = lambda x: jnp.transpose(x.reshape(3, 3, K, K), (2, 3, 0, 1))
    return (
        out_map,
        grad_band.T,
        grad_cols.T,
        grad_w_row.T,
        grad_w_col.T,
        unfold(grad_one),
        unfold(grad_two),
    )


def solution(mesh):
    placed = (
        P("row", "col"),
        P("col", "row"),
        P(),
        P(),
        P(),
        P(),
        P(None, "row", "col"),
        P("row", "col"),
        P("row", "col"),
        P(),
    )
    return jax.shard_map(
        per_device,
        mesh=mesh,
        in_specs=placed,
        out_specs=(P(None, "row", "col"), P("row", "col"), P("col", "row"), P(), P(), P(), P()),
        check_vma=False,
    )
```

```python
import functools

import jax
import jax.numpy as jnp
from jax import lax
from jax.experimental import pallas as pl
from jax.experimental.pallas import tpu as pltpu
from jax.sharding import PartitionSpec as P

tanh_scale = 0.7978845608028654
cubic_term = 0.044715
keep_boost = 4.0 / 3.0
slope_cubic = 3.0 * tanh_scale * cubic_term

K = 32
ROWS = 16
COLS = 512
WIDE = 640
TAPS = 9
BLK = 8 * K
HIGH = lax.Precision.HIGHEST
f32 = jnp.float32
bf16 = jnp.bfloat16


def dot(a, b, precision=None):
    return lax.dot_general(
        a, b, (((1,), (0,)), ((), ())), precision=precision, preferred_element_type=f32
    )


def dot_nt(a, b, precision=None):
    return lax.dot_general(
        a, b, (((1,), (1,)), ((), ())), precision=precision, preferred_element_type=f32
    )


def dot_tn(a, b, precision=None):
    return lax.dot_general(
        a, b, (((0,), (0,)), ((), ())), precision=precision, preferred_element_type=f32
    )


def split(x):
    high = x.astype(bf16)
    return high, (x - high.astype(f32)).astype(bf16)


def fine(product, exact, x):
    high, low = split(x)
    return product(exact, high) + product(exact, low)


def fine_nt(a, b):
    a_high, a_low = split(a)
    b_high, b_low = split(b)
    return dot_nt(a_high, b_high) + (dot_nt(a_high, b_low) + dot_nt(a_low, b_high))


def iota(shape, dim):
    return lax.broadcasted_iota(jnp.int32, shape, dim)


def ahead(x, s):
    lane = iota((x.shape[0], 128), 1)
    turned = [pltpu.roll(x[:, i : i + 128], 128 - s, 1) for i in range(0, x.shape[1], 128)]
    nxt = turned[1:] + turned[:1]
    return jnp.concatenate(
        [jnp.where(lane >= 128 - s, n, t) for t, n in zip(turned, nxt)], axis=1
    )


def behind(x, s):
    lane = iota((x.shape[0], 128), 1)
    turned = [pltpu.roll(x[:, i : i + 128], s, 1) for i in range(0, x.shape[1], 128)]
    prv = turned[-1:] + turned[:-1]
    return jnp.concatenate([jnp.where(lane < s, p, t) for t, p in zip(turned, prv)], axis=1)


def mixed(base, factor):
    h = base * 668265261
    h = h ^ lax.shift_right_logical(h, 15)
    h = h * 374761393
    h = h ^ lax.shift_right_logical(h, 13)
    return jnp.where((h & 3) != 0, factor, 0.0)


def wrapped(number):
    return (number + 2**31) % 2**32 - 2**31


def gelu_parts(v):
    v2 = v * v
    t = jnp.tanh(v * (tanh_scale + (tanh_scale * cubic_term) * v2))
    p = 0.5 + 0.5 * t
    value = v * p
    slope = p + value * (1.0 - t) * (tanh_scale + slope_cubic * v2)
    return value, slope


def first_kernel(seed_ref, mask_ref, cols_ref, band_ref, cot_first_ref, cot_last_ref, out_ref):
    out_ref[0:32, :] = cols_ref[...]
    lane = iota((8, 128), 1)
    seed = seed_ref[0, 0]
    bytes_of = [seed >> 16 & 255, seed >> 8 & 255, seed & 255, mask_ref[0, 0]]
    numbers = jnp.zeros((8, 128), jnp.int32)
    for i, value in enumerate(bytes_of):
        numbers = jnp.where(lane == i, value, numbers)
    band = jnp.concatenate([band_ref[...].astype(f32), jnp.zeros((8, 112), f32)], axis=1)
    out_ref[32:48, 0:128] = jnp.concatenate([band, numbers.astype(f32)], axis=0).astype(bf16)
    out_ref[32:48, 128:] = jnp.zeros((16, COLS - 128), bf16)
    lane = iota((16, 128), 1)
    for side, cot_ref, shift in ((0, cot_first_ref, 0), (1, cot_last_ref, 8)):
        for half in range(2):
            total = jnp.zeros((16, 128), f32)
            for i in range(16):
                piece = cot_ref[16 * half + i].astype(f32)
                turn = (8 * i + shift) % 128
                piece = pltpu.roll(piece, turn, 1) if turn else piece
                here = jnp.logical_and(lane >= 8 * i, lane < 8 * i + 8)
                total = jnp.where(here, piece, total)
            at = 256 * side + 128 * half
            out_ref[48:64, at : at + 128] = total.astype(bf16)


def pack_kernel(
    own_ref, one_ref, two_ref, three_ref, other_ref,
    feats_ref, first_ref, second_ref, bands_ref,
):
    even = lax.rem(lax.axis_index("row"), 2) == 0
    lane = iota((32, 128), 1)
    mine = [own_ref, one_ref, two_ref, three_ref]
    west = jnp.zeros((32, 128), f32)
    east = jnp.zeros((32, 128), f32)
    bands = jnp.zeros((8, 128), f32)
    seeds = jnp.zeros((8, 128), f32)
    edges = []
    for t in range(8):
        a = mine[t // 2]
        b = other_ref.at[t // 2]
        if t % 2 == 0:
            pick = lambda rows, cols: jnp.where(even, a[rows, cols], b[rows, cols])
        else:
            pick = lambda rows, cols: jnp.where(even, b[rows, cols], a[rows, cols])
        feats_ref[t] = pick(slice(0, 32), slice(0, COLS))
        here = jnp.logical_and(lane >= 16 * t, lane < 16 * t + 16)
        first = pick(slice(0, 32), slice(0, 128)).astype(f32)
        west = jnp.where(here, pltpu.roll(first, 16 * t, 1) if t else first, west)
        last = pick(slice(0, 32), slice(COLS - 128, COLS)).astype(f32)
        turn = (16 * t + 16) % 128
        east = jnp.where(here, pltpu.roll(last, turn, 1) if turn else last, east)
        edges.append(pick(slice(48, 64), slice(0, COLS)).astype(f32) if t in (0, 1, 2, 7) else None)
        extra = pick(slice(32, 48), slice(0, 128)).astype(f32)
        extra = pltpu.roll(extra, 16 * t, 1) if t else extra
        bands = jnp.where(here[:8], extra[0:8], bands)
        seeds = jnp.where(here[:8], extra[8:16], seeds)
    blank = jnp.zeros((8, 128), f32)
    tail = jnp.concatenate([seeds, blank], axis=0).astype(bf16)
    around = [edges[7], edges[0], edges[1]], [edges[0], edges[1], edges[2]]
    three = [jnp.where(even, x, y) for x, y in zip(*around)]
    rows = jnp.concatenate([three[0][8:16], three[1], three[2][0:8]], axis=0).astype(bf16)
    whole = []
    for value, at in ((west, 0), (east, 256)):
        halves = [rows[:, at : at + 128], rows[:, at + 128 : at + 256]]
        whole.append(jnp.concatenate([value.astype(bf16)] + halves + [tail], axis=0))
    even_col = lax.rem(lax.axis_index("col"), 2) == 0
    first_ref[...] = jnp.where(even_col, whole[1], whole[0])
    second_ref[...] = jnp.where(even_col, whole[0], whole[1])
    bands_ref[...] = jnp.broadcast_to(bands.astype(bf16)[None], (32, 8, 128))


def main_kernel(
    place,
    feats_ref,
    bands_ref,
    own_ref,
    one_ref,
    two_ref,
    wr_ref,
    wc_ref,
    w1_ref,
    w2_ref,
    cot_ref,
    inner_ref,
    outer_ref,
    out_ref,
    send_ref,
    t1,
    t2,
    t2m,
    zv,
    gk,
    xv,
    hv,
    gv,
    g1,
    d1,
    acc,
    first_out,
    row_all,
    row3,
    keep_rows,
    seed_rows,
    base_ref,
    keep_ref,
    cot_halo,
    every,
):
    s1 = place[0]
    s2 = place[1]
    r = lax.axis_index("row")
    c = lax.axis_index("col")
    turn = r // 2
    even_col = lax.rem(c, 2) == 0
    right_all = jnp.where(even_col, one_ref[...], two_ref[...])
    left_all = jnp.where(even_col, two_ref[...], one_ref[...])

    spread = (iota((K, BLK), 1) // 8 == iota((K, BLK), 0)).astype(f32).astype(bf16)
    sub = iota((8, BLK), 0)
    far = iota((8, BLK), 1) % 8 - sub

    def hits(s, half):
        return [far + 8 * half == 4 + (a - 1) * s for a in range(3)]

    def build(target, weight, s, mirrored, by_tap=False):
        masks = [hits(s, half) for half in range(2)]
        for b in range(3):
            grown = []
            for a in range(3):
                if mirrored:
                    grown.append(dot_tn(weight[(2 - a) * 3 + (2 - b)], spread))
                else:
                    grown.append(dot(weight[a * 3 + b], spread))
            for half in range(2):
                m = masks[half]
                whole = jnp.zeros((K, 8, BLK), f32)
                for a in range(3):
                    whole = jnp.where(
                        jnp.broadcast_to(m[a][None], (K, 8, BLK)),
                        jnp.broadcast_to(grown[a][:, None, :], (K, 8, BLK)),
                        whole,
                    )
                at = (b * 2 + half if by_tap else half * 3 + b) * BLK
                target[:, at : at + BLK] = whole.reshape(BLK, BLK).astype(bf16)

    build(t1, w1_ref, s1, False, True)
    build(t2, w2_ref, s2, False)
    build(t2m, w2_ref, s2, True)

    lane = iota((K, 128), 1)
    right = right_all[0:32].astype(f32)
    left = left_all[0:32].astype(f32)
    for t in range(8):
        r_turn = (128 - 16 * t) % 128
        l_turn = (112 - 16 * t) % 128
        halo = jnp.where(
            lane < 64,
            pltpu.roll(right, r_turn, 1) if r_turn else right,
            pltpu.roll(left, l_turn, 1) if l_turn else left,
        ).astype(bf16)
        every[32 * t : 32 * t + 32, 0:COLS] = feats_ref[t]
        every[32 * t : 32 * t + 32, COLS:] = halo
    weight = pltpu.roll(wc_ref[...].astype(f32), lax.rem(256 - 64 * turn, 256), 1).astype(bf16)
    q = dot(weight, every[...])
    place_of = jnp.where(iota((1, WIDE), 1) < COLS, 0, jnp.where(iota((1, WIDE), 1) < 576, 1, 2))
    tile_of = [(place_of == m).astype(f32) for m in range(3)]
    ones = jnp.zeros((K, WIDE), f32)
    for m in range(3):
        row = iota((K, WIDE), 0)
        ones = jnp.where(jnp.logical_or(row == m, row == m + 3), tile_of[m], ones)
    q_rest = q - q.astype(bf16).astype(f32)
    for b, move in enumerate((behind, lambda x, s: x, ahead)):
        moved = move(q, s1)
        flags = move(ones, s1)
        for m in range(3):
            at = 128 * b + K * m
            xv[at : at + K, :] = (moved * flags[m : m + 1]).astype(bf16)
        xv[128 * b + 96 : 128 * b + 128, :] = flags.astype(bf16)
        xv[384 + K * b : 384 + K * b + K, :] = (move(q_rest, s1) * flags[0:1]).astype(bf16)
        xv[512 + K * b : 512 + K * b + K, :] = xv[128 * b : 128 * b + K, :]
    xv[480:512, :] = jnp.zeros((K, WIDE), bf16)
    xv[608:640, :] = jnp.zeros((K, WIDE), bf16)

    bands = bands_ref[...].astype(f32)[:, 0:8, :].reshape(256, 128).astype(bf16)
    row_t = dot(wr_ref[...], bands)
    row_all[...] = row_t.T
    core = lax.rem(r, 2)
    lane128 = iota((1, 128), 1)
    row_t = pltpu.roll(row_t, lax.rem(128 - 16 * core, 128), 1)
    row_t = jnp.where(lane128 < 16, row_t, 0.0)

    lane = iota((1, WIDE), 1)
    for step in range(3):
        slot = lax.rem(core + step + 7, 8)
        row3[16 * step : 16 * step + 16, :] = row_all[
            pl.ds(pl.multiple_of(16 * slot, 16), 16), :
        ]
        sides = []
        for edge in (own_ref[...], right_all, left_all):
            piece = edge[96:112].astype(f32)[0:1]
            piece = pltpu.roll(piece, lax.rem(128 - 16 * slot, 128), 1)
            number = piece[:, 0:1] * 65536.0 + piece[:, 1:2] * 256.0 + piece[:, 2:3]
            sides.append((number, piece[:, 3:4]))
        row_ok = jnp.logical_and(r + step >= 1, r + step <= 8).astype(f32)
        right_ok = row_ok * (c < 31).astype(f32)
        left_ok = row_ok * (c > 0).astype(f32)
        keep = jnp.where(
            lane < COLS,
            sides[0][1] * row_ok,
            jnp.where(lane < 576, sides[1][1] * right_ok, sides[2][1] * left_ok),
        )
        seed = jnp.where(
            lane < COLS, sides[0][0], jnp.where(lane < 576, sides[1][0], sides[2][0])
        )
        seed_rows[step] = seed.astype(jnp.int32)
        keep_rows[step] = keep

    lane32 = iota((32, 128), 1)
    for ch in range(K):
        first = 32 + ch // 16 * 32
        right = right_all[first : first + 32].astype(f32)
        left = left_all[first : first + 32].astype(f32)
        r_turn = (128 - 8 * ch) % 128
        l_turn = (120 - 8 * ch) % 128
        cot_halo[32 * ch : 32 * ch + 32, :] = jnp.where(
            lane32 < 64,
            pltpu.roll(right, r_turn, 1) if r_turn else right,
            pltpu.roll(left, l_turn, 1) if l_turn else left,
        )

    column = iota((8, WIDE), 1)
    column = c * COLS + jnp.where(column < 576, column, column - WIDE)

    def prepare(first_row, layer):
        local = first_row + iota((8, WIDE), 0)
        seed = jnp.where(
            local < 0, seed_rows[0], jnp.where(local < ROWS, seed_rows[1], seed_rows[2])
        )
        keep = jnp.where(
            local < 0, keep_rows[0], jnp.where(local < ROWS, keep_rows[1], keep_rows[2])
        )
        base = seed * 1000003 + layer * 7919
        base = base ^ ((r * ROWS + local) * 19349663)
        base_ref[...] = base ^ (column * 83492791)
        keep_ref[...] = keep * keep_boost

    def factor_of(p):
        keep = keep_ref[...]
        base = base_ref[...]
        parts = [mixed(base ^ wrapped(ch * 73856093), keep) for ch in (2 * p, 2 * p + 1)]
        return jnp.concatenate(parts, axis=0)

    def store_shifted(target, block, p, values, s):
        values = values.astype(bf16)
        for b, moved in enumerate((behind(values, s), values, ahead(values, s))):
            at = pl.multiple_of(block * 3 * BLK + b * BLK + 16 * p, 16)
            target[pl.ds(at, 16), :] = moved

    lane_m = jnp.where(lane128 < 96, lane128 // K, lane128 - 96)
    for k in range(6):
        rows = row3[8 * k : 8 * k + 8, :]
        keep = keep_rows[k // 2]
        keep = jnp.where(
            lane_m == 0,
            keep[:, 0:1],
            jnp.where(lane_m == 1, keep[:, COLS : COLS + 1], keep[:, WIDE - 1 : WIDE]),
        )
        keep = jnp.where(lane_m < 3, keep, 0.0)
        for p in range(K // 2):
            parts = []
            for ch in (2 * p, 2 * p + 1):
                picked = jnp.where(lane128 % K == ch, keep, 0.0)
                parts.append(jnp.where(lane128 < 96, picked, keep * rows[:, ch : ch + 1]))
            at = k * BLK + 16 * p
            zv[at : at + 16, :] = jnp.concatenate(parts, axis=0).astype(bf16)
    for k in (0, 2, 4):
        both = zv[k * BLK : (k + 2) * BLK, :]
        if k < 4:
            both = jnp.concatenate([both, zv[(k + 1) * BLK : (k + 3) * BLK, :]], axis=1)
        taps = [dot(t1[:, 2 * BLK * b : 2 * BLK * (b + 1)], both) for b in range(3)]
        for i in range(2 if k < 4 else 1):
            own_tile = jnp.zeros((BLK, 128), f32)
            for b in range(3):
                found = taps[b][:, 128 * i : 128 * i + 128]
                rest = found - found.astype(bf16).astype(f32)
                rest = jnp.where(jnp.logical_and(lane128 >= 99, lane128 < 102), pltpu.roll(rest, 3, 1), found)
                gk[k + i, :, 128 * b : 128 * b + 128] = rest.astype(bf16)
                here = jnp.logical_and(lane128 >= K * b, lane128 < K * b + K)
                own_tile = jnp.where(here, pltpu.roll(found, K * b, 1) if b else found, own_tile)
            rounded = own_tile.astype(bf16)
            gk[k + i, :, 384:512] = rounded
            gk[k + i, :, 512:640] = (own_tile - rounded.astype(f32)).astype(bf16)

    def convolve(k, weight, values, to):
        acc[to] = dot(weight[...], values[k * 3 * BLK : (k + 2) * 3 * BLK, :])

    def hidden_block(k, at_acc):
        prepare(8 * k - 12, 1)
        for p in range(K // 2):
            at = 16 * p
            value, slope = gelu_parts(acc[at_acc, at : at + 16, :])
            factor = factor_of(p)
            store_shifted(hv, k, p, factor * value, s2)
            if 1 <= k <= 3:
                d1[(k - 1) * BLK + at : (k - 1) * BLK + at + 16, :] = factor * slope

    def grad_block(k, at_acc):
        prepare(8 * k - 8, 2)
        for p in range(K // 2):
            at = 16 * p
            value, slope = gelu_parts(acc[at_acc, at : at + 16, :])
            factor = factor_of(p)
            if k == 0:
                cot = jnp.where(core == 0, outer_ref[at : at + 16, :], inner_ref[at : at + 16, :])
                cot = cot.astype(f32)
            elif k == 3:
                cot = jnp.where(core == 0, inner_ref[at : at + 16, :], outer_ref[at : at + 16, :])
                cot = cot.astype(f32)
            else:
                parts = []
                for ch in (2 * p, 2 * p + 1):
                    parts.append(cot_ref[ch].astype(f32)[8 * (k - 1) : 8 * k])
                cot = jnp.concatenate(parts, axis=0)
            halo = []
            for i in range(2):
                first = 64 * p + 32 * i + 8 * k
                halo.append(cot_halo[first : first + 8, :])
            cot = jnp.concatenate([cot, jnp.concatenate(halo, axis=0)], axis=1)
            store_shifted(gv, k, p, cot * factor * slope, s2)
            if k == 1:
                first_out[at : at + 16, :] = (factor * value)[:, :COLS]
            if k == 2:
                upper = first_out[at : at + 16, :]
                lower = (factor * value)[:, :COLS]
                for i in range(2):
                    both = jnp.concatenate(
                        [upper[8 * i : 8 * i + 8], lower[8 * i : 8 * i + 8]], axis=0
                    )
                    out_ref[2 * p + i] = both.astype(bf16)

    def back_block(k, at_acc):
        g1[k * BLK : (k + 1) * BLK, :] = (
            acc[at_acc] * d1[k * BLK : (k + 1) * BLK, :]
        ).astype(bf16)

    def convolve_first(k, weight, values, to):
        acc[to] = dot(weight[k], values[...])

    jobs = [(convolve_first, k, gk, xv, functools.partial(hidden_block, k)) for k in range(5)]
    jobs += [(convolve, k, t2, hv, functools.partial(grad_block, k)) for k in range(4)]
    jobs += [(convolve, k, t2m, gv, functools.partial(back_block, k)) for k in range(3)]
    for i, (start, k, weight, values, _) in enumerate(jobs):
        start(k, weight, values, i % 2)
        if i:
            jobs[i - 1][4]((i - 1) % 2)
    jobs[-1][4]((len(jobs) - 1) % 2)

    crossed = []
    for half in range(2):
        total = jnp.zeros((BLK, 3 * BLK), f32)
        for k in (1, 2):
            start = k * 3 * BLK + BLK
            grads = gv[start : start + BLK, 0:COLS]
            start = (k + half) * 3 * BLK
            total = total + dot_nt(grads, hv[start : start + 3 * BLK, 0:COLS])
        crossed.append(total)
    gather8 = (iota((3 * BLK, 96), 0) // 8 == iota((3 * BLK, 96), 1)).astype(f32).astype(bf16)
    offset = iota((8, 3 * BLK), 1) % 8 - iota((8, 3 * BLK), 0)
    folded = []
    for a in range(3):
        found = jnp.zeros((K, 8, 3 * BLK), f32)
        for half in range(2):
            m = offset + 8 * half == 4 + (a - 1) * s2
            found = jnp.where(
                jnp.broadcast_to(m[None], found.shape), crossed[half].reshape(found.shape), found
            )
        folded.append(jnp.sum(found, axis=1))
    folded = jnp.concatenate(folded, axis=0)
    second_total = fine(lambda e, x: dot(x, e), gather8, folded)

    place_j = iota((WIDE, 128), 0)
    place_j = jnp.where(place_j < 576, place_j, place_j - WIDE)
    which = iota((3 * BLK, 128), 0)
    which = iota((3 * BLK, 128), 1) == which // BLK * 8 + which % 8
    same = (iota((K, 3 * BLK), 1) % BLK // 8 == iota((K, 3 * BLK), 0)).astype(f32).astype(bf16)
    by_row = []
    for b in range(3):
        moved_j = place_j + (b - 1) * s1
        window = jnp.logical_and(moved_j >= 0, moved_j < COLS).astype(f32).astype(bf16)
        by_row.append(fine(dot, same, jnp.where(which, dot(g1[...], window), 0.0)))
    across = iota((96, 3 * BLK), 1)
    down = iota((96, 3 * BLK), 0)
    moved_i = across // BLK * 8 + across % 8 - 4 + (down // K - 1) * s1
    inside = jnp.logical_and(moved_i >= 0, moved_i < ROWS)
    inside = jnp.logical_and(inside, across % BLK // 8 == down % K)
    by_col = dot(inside.astype(f32).astype(bf16), g1[...])
    by_col = jnp.concatenate([ahead(by_col, s1), by_col, behind(by_col, s1)], axis=0)

    keep_own = keep_rows[1][:, 0:1]
    weights = [w1_ref[a * 3 + b] for b in range(3) for a in range(3)]
    col_sum = fine(dot_tn, jnp.concatenate(weights, axis=0), by_col)
    row_sum = jnp.zeros((K, 128), f32)
    turned = []
    for a in range(3):
        turns = 128 - (4 - (a - 1) * s1)
        flat = jnp.concatenate([w1_ref[a * 3 + b] for b in range(3)], axis=0)
        row_sum = row_sum + pltpu.roll(
            fine(dot_tn, flat, jnp.concatenate(by_row, axis=0)), turns, 1
        )
        turned.append([pltpu.roll(by_row[b], turns, 1) for b in range(3)])
    turned = jnp.concatenate([turned[a][b] for b in range(3) for a in range(3)], axis=0)
    first_all = fine_nt(by_col[:, :COLS], q[:, :COLS]) + fine_nt(turned, row_t)
    first_total = jnp.concatenate([first_all[96 * b : 96 * b + 96] for b in range(3)], axis=1)
    first_total = first_total * keep_own
    row_sum = jnp.where(lane128 < 16, row_sum * keep_own, 0.0)
    row_sum = pltpu.roll(row_sum, 16 * r, 1)

    col_sum = col_sum * keep_own
    for g in range(4):
        send_ref[32 * g : 32 * g + 32, :] = col_sum[:, 128 * g : 128 * g + 128].astype(bf16)
    send_ref[128:224, :] = jnp.concatenate([first_total, second_total[:, 0:32]], axis=1).astype(bf16)
    send_ref[224:272, :] = jnp.concatenate(
        [second_total[0:48, 32:96], second_total[48:96, 32:96]], axis=1
    ).astype(bf16)
    send_ref[272:304, :] = row_sum.astype(bf16)


def four(own_ref, a_ref, b_ref, c_ref):
    pair = own_ref[...].astype(f32) + b_ref[...].astype(f32)
    return pair + (a_ref[...].astype(f32) + c_ref[...].astype(f32))


def middle_kernel(
    own_ref, a_ref, b_ref, c_ref, feats_ref, wc_ref, gcols_ref, send_ref
):
    r = lax.axis_index("row")
    total = four(own_ref, a_ref, b_ref, c_ref)
    weight = pltpu.roll(wc_ref[...].astype(f32), lax.rem(256 - 32 * r, 256), 1)
    weight = weight[:, 0:K].astype(bf16)
    grad_w = jnp.zeros((K, 256), f32)
    for g in range(4):
        part = total[32 * g : 32 * g + 32, :]
        gcols_ref[:, 128 * g : 128 * g + 128] = fine(dot_tn, weight, part).astype(bf16)
        seen = feats_ref[:, :, 128 * g : 128 * g + 128].reshape(256, 128)
        grad_w = grad_w + fine(lambda e, x: dot_nt(x, e), seen, part)
    grad_w = pltpu.roll(grad_w, 64 * (r // 2), 1)
    send_ref[0:176, :] = total[128:304].astype(bf16)
    send_ref[176:208, :] = grad_w[:, 0:128].astype(bf16)
    send_ref[208:240, :] = grad_w[:, 128:256].astype(bf16)


def last_kernel(
    own_ref, a_ref, bands_ref, wr_ref, gband_ref, gwr_ref, gwc_ref, g1_ref, g2_ref
):
    r = lax.axis_index("row")
    c = lax.axis_index("col")
    total = own_ref[...].astype(f32) + a_ref[...].astype(f32)
    rest = jnp.concatenate([total[96:144, 0:64], total[96:144, 64:128]], axis=0)
    for a in range(3):
        for b in range(3):
            g1_ref[a * 3 + b] = total[32 * a : 32 * a + 32, 32 * b : 32 * b + 32]
        g2_ref[a * 3] = total[32 * a : 32 * a + 32, 96:128]
        g2_ref[a * 3 + 1] = rest[32 * a : 32 * a + 32, 0:32]
        g2_ref[a * 3 + 2] = rest[32 * a : 32 * a + 32, 32:64]
    rows = total[144:176, :]
    gwc_ref[:, 0:128] = total[176:208]
    gwc_ref[:, 128:256] = total[208:240]
    bands = bands_ref[...].astype(f32)[:, 0:8, :].reshape(256, 128)
    turned = pltpu.roll(rows, lax.rem(128 - 32 * (r // 2), 128), 1)
    gwr_ref[...] = fine(lambda e, x: dot_nt(x, e), bands.astype(bf16), turned)
    mine = pltpu.roll(wr_ref[...].astype(f32), lax.rem(256 - 8 * c, 256), 1)[:, 0:128]
    mine = fine(dot_tn, mine.astype(bf16), pltpu.roll(rows, lax.rem(128 - 16 * r, 128), 1))
    gband_ref[...] = mine[0:8, 0:16].astype(bf16)


def call(kernel, shapes, args, scratch=(), scalars=0, limit=8, blocks={}):
    whole = pl.BlockSpec(memory_space=pltpu.VMEM)
    specs = [pl.BlockSpec(memory_space=pltpu.SMEM)] * scalars
    specs += [whole] * (len(args) - scalars)
    for i, (dims, at) in blocks.items():
        specs[i] = pl.BlockSpec(dims, lambda _, at=at: at)
    return pl.pallas_call(
        kernel,
        out_shape=shapes,
        grid=(1,) if blocks else (),
        in_specs=specs,
        out_specs=jax.tree.map(lambda _: whole, shapes),
        scratch_shapes=list(scratch),
        compiler_params=pltpu.CompilerParams(vmem_limit_bytes=limit * 1024 * 1024),
    )(*args)


def shape(dims, kind):
    return jax.ShapeDtypeStruct(dims, kind)


def per_device(
    band_emb,
    col_emb,
    w_row,
    w_col,
    first_kernel_weight,
    second_kernel_weight,
    cotangent,
    drop_seeds,
    tile_mask,
    dilations,
):
    rows = lax.axis_size("row")
    cols = lax.axis_size("col")

    cols_t = col_emb.T
    own = call(
        first_kernel,
        shape((64, COLS), bf16),
        (drop_seeds, tile_mask, cols_t, band_emb.T, cotangent, cotangent),
        blocks={4: ((K, ROWS, 128), (0, 0, 0)), 5: ((K, ROWS, 128), (0, 0, COLS // 128 - 1))},
        scalars=2,
    )
    beyond = [
        lax.ppermute(own, "row", [((i + 2 * s) % rows, i) for i in range(rows)]) for s in (1, 2, 3)
    ]
    flip = [(i, i ^ 1) for i in range(rows)]
    other = lax.ppermute(jnp.stack([own] + beyond), "row", flip)

    feats, edge_first, edge_second, bands = call(
        pack_kernel,
        (
            shape((8, K, COLS), bf16),
            shape((112, 128), bf16),
            shape((112, 128), bf16),
            shape((32, 8, 128), bf16),
        ),
        (own, *beyond, other),
    )
    inside = [(i, i ^ 1) for i in range(cols)]
    between = [(i, (i + 1 if i % 2 else i - 1) % cols) for i in range(cols)]
    edge_one = lax.ppermute(edge_first, "col", inside)
    edge_two = lax.ppermute(edge_second, "col", between)
    bands = lax.all_to_all(bands, "col", 0, 0)

    core = lax.rem(lax.axis_index("row"), 2)
    inner = lax.dynamic_slice_in_dim(cotangent, 8 * (1 - core), 8, 1)
    outer = lax.dynamic_slice_in_dim(cotangent, 8 * core, 8, 1)
    pairs = [(i, (i + 1 if i % 2 else i - 1) % rows) for i in range(rows)]
    inner = lax.ppermute(inner, "row", flip).reshape(BLK, COLS)
    outer = lax.ppermute(outer, "row", pairs).reshape(BLK, COLS)

    w1 = jnp.transpose(first_kernel_weight, (2, 3, 0, 1)).reshape(TAPS, K, K)
    w2 = jnp.transpose(second_kernel_weight, (2, 3, 0, 1)).reshape(TAPS, K, K)
    out_map, sums = call(
        main_kernel,
        (shape((K, ROWS, COLS), bf16), shape((304, 128), bf16)),
        (
            dilations,
            feats,
            bands,
            edge_first,
            edge_one,
            edge_two,
            w_row.T,
            w_col.T,
            w1,
            w2,
            cotangent,
            inner,
            outer,
        ),
        scratch=(
            pltpu.VMEM((BLK, 6 * BLK), bf16),
            pltpu.VMEM((BLK, 6 * BLK), bf16),
            pltpu.VMEM((BLK, 6 * BLK), bf16),
            pltpu.VMEM((6 * BLK, 128), bf16),
            pltpu.VMEM((5, BLK, 640), bf16),
            pltpu.VMEM((640, WIDE), bf16),
            pltpu.VMEM((15 * BLK, WIDE), bf16),
            pltpu.VMEM((12 * BLK, WIDE), bf16),
            pltpu.VMEM((3 * BLK, WIDE), bf16),
            pltpu.VMEM((3 * BLK, WIDE), f32),
            pltpu.VMEM((2, BLK, WIDE), f32),
            pltpu.VMEM((BLK, COLS), f32),
            pltpu.VMEM((128, K), f32),
            pltpu.VMEM((48, K), f32),
            pltpu.VMEM((3, 1, WIDE), f32),
            pltpu.VMEM((3, 1, WIDE), jnp.int32),
            pltpu.VMEM((8, WIDE), jnp.int32),
            pltpu.VMEM((8, WIDE), f32),
            pltpu.VMEM((32 * K, 128), f32),
            pltpu.VMEM((8 * K, WIDE), bf16),
        ),
        scalars=1,
        limit=44,
    )

    def added(x, y):
        return (x.astype(f32) + y.astype(f32)).astype(bf16)

    def quarters(x, axis, count, place):
        step, size = place
        turned = lambda i, s: i - i // step % size * step + (i // step + s) % size * step
        return [
            lax.ppermute(x, axis, [(i, turned(i, s)) for i in range(count)]) for s in (1, 2, 3)
        ]

    sums = added(sums, lax.ppermute(sums, "row", flip))
    grad_cols, terms = call(
        middle_kernel,
        (shape((K, COLS), bf16), shape((240, 128), bf16)),
        (sums, *quarters(sums, "row", rows, (2, 4)), feats, w_col.T),
    )
    for place in ((1, 4), (4, 4)):
        one, two, three = quarters(terms, "col", cols, place)
        pair = terms.astype(f32) + two.astype(f32)
        terms = (pair + (one.astype(f32) + three.astype(f32))).astype(bf16)
    grad_band, grad_w_row, grad_w_col, grad_one, grad_two = call(
        last_kernel,
        (
            shape((8, ROWS), bf16),
            shape((K, 256), f32),
            shape((K, 256), f32),
            shape((TAPS, K, K), f32),
            shape((TAPS, K, K), f32),
        ),
        (
            terms,
            lax.ppermute(terms, "col", [(i, (i + 16) % cols) for i in range(cols)]),
            bands,
            w_row.T,
        ),
    )
    unfold = lambda x: jnp.transpose(x.reshape(3, 3, K, K), (2, 3, 0, 1))
    return (
        out_map,
        grad_band.T,
        grad_cols.T,
        grad_w_row.T,
        grad_w_col.T,
        unfold(grad_one),
        unfold(grad_two),
    )


def solution(mesh):
    placed = (
        P("row", "col"),
        P("col", "row"),
        P(),
        P(),
        P(),
        P(),
        P(None, "row", "col"),
        P("row", "col"),
        P("row", "col"),
        P(),
    )
    return jax.shard_map(
        per_device,
        mesh=mesh,
        in_specs=placed,
        out_specs=(P(None, "row", "col"), P("row", "col"), P("col", "row"), P(), P(), P(), P()),
        check_vma=False,
    )
```
